128 devices in a mesh: dp: 16 (over y_hi, x, core), expert: 8 (over z, y_lo).
Axes of the slice: x: 4, y: 4 (y_hi: 2, y_lo: 2; y = y_hi * 2 + y_lo), z: 4, core: 2. Of those that a mesh axis runs over, the one named last changes fastest.
Arguments:
- tokens: bfloat16 [4096, 4, 4096], P(('dp', 'expert')), may hold values from -6 to 6
- cotangent: bfloat16 [4096, 4, 4096], P(('dp', 'expert')), may hold values from -6 to 6
- group_of: int32 [4096, 4], P(('dp', 'expert')), may hold values from 0 to 127, as said below
- mixer: bfloat16 [4096, 32], replicated, may hold values from -0.1875 to 0.1875
- w_in: bfloat16 [32, 4096, 2048], P('dp', None, 'expert'), may hold values from -0.09375 to 0.09375
- w_out: bfloat16 [32, 2048, 4096], P('dp', 'expert'), may hold values from -0.125 to 0.125
Outputs:
- grad_tokens: bfloat16 [4096, 4, 4096], P(('dp', 'expert'))
- grad_mixer: float32 [4096, 32], replicated
- grad_in: bfloat16 [32, 4096, 2048], P('dp', None, 'expert')
- grad_out: bfloat16 [32, 2048, 4096], P('dp', 'expert')
The draws below stay inside these ranges and needn't reach their ends.
Inputs may be any that keep to these rules, and one draw needn't show every extreme that they name: `group_of`: sequences lie on devices in the order of dp, then expert. Group number q lies on the devices whose expert index is q // 16; at each position it takes exactly 2 sequences of each of them, so every group has 32 members.
All inputs are finite; a program needn't handle non-finite values.
Results may differ from the reference program's by a relative error of at most 0.024.
Values may be sent and summed in bfloat16 or wider, within the bound.
No kernel may reach another device: no remote copies, remote signals or barrier semaphores. Data moves between devices by JAX's collectives and lax.ppermute only.
A program may use at most 192 MiB of HBM per device.

```python
import jax
import jax.numpy as jnp
from jax import lax

D = 4096
FF = 2048
GROUP = 32
POSITIONS = 4
EXPERTS = 32
SEQ_DEV = 32
SEQS = 4096
MEMBERS = 2
N_DP = 16
N_EXPERT = 8
DEVICES = 128


def draw_group_of(key, part):
    key = jax.random.fold_in(key, 7)
    keys = jax.random.split(key, POSITIONS * DEVICES)
    base = jnp.arange(SEQ_DEV, dtype=jnp.int32) // MEMBERS
    shuffled = jax.vmap(lambda single: jax.random.permutation(single, base))(keys)
    shuffled = shuffled.reshape(POSITIONS, N_DP, N_EXPERT, SEQ_DEV)
    offset = (jnp.arange(N_EXPERT, dtype=jnp.int32) * N_DP)[None, None, :, None]
    values = (shuffled + offset).reshape(POSITIONS, SEQS)
    return values.T.astype(jnp.int32)


def levels(rng, shape, cuts, low, high):
    def one(axis_at, blocks):
        steps = jax.random.uniform(jax.random.fold_in(jax.random.fold_in(rng, 6), axis_at), (blocks,), jnp.float32, low / len(cuts), high / len(cuts))
        return jnp.repeat(jnp.exp(steps), shape[axis_at] // blocks).reshape((-1,) + (1,) * (len(shape) - axis_at - 1))

    gain = one(*cuts[0])
    for cut in cuts[1:]:
        gain = gain * one(*cut)
    return gain


def scatter_about(stream_key, dims, width, most, shards=(), kind=jnp.bfloat16):
    drawn = jax.random.normal(stream_key, dims, jnp.float32) * width
    if len(shards) > 0:
        drawn = levels(stream_key, dims, shards, -0.22, 0.18) * drawn
    return jnp.clip(drawn, min=-most, max=most).astype(kind)


def setup_inputs(seed: int = 0) -> dict:
    seeds = jax.random.split(jax.random.key(seed), 7)
    return {
        "tokens": scatter_about(seeds[0], (SEQS, POSITIONS, D), 1.0, 6.0, ((0, 128),)),
        "cotangent": scatter_about(seeds[1], (SEQS, POSITIONS, D), 1.0, 6.0, ((0, 128),)),
        "group_of": draw_group_of(jax.random.fold_in(seeds[6], 71), 0),
        "mixer": scatter_about(seeds[3], (D, EXPERTS), (D // 4) ** -0.5, 0.1875),
        "w_in": scatter_about(seeds[4], (EXPERTS, D, FF), D ** -0.5, 0.09375, ((0, 16), (2, 8))),
        "w_out": scatter_about(seeds[5], (EXPERTS, FF, D), FF ** -0.5, 0.125, ((0, 16), (1, 8))),
    }


soft_cap = 15.0


def shard_sums(left, right_w, form):
    parts = jnp.einsum(form, left.astype(jnp.float32), right_w.astype(jnp.float32))
    rounded = lax.optimization_barrier(parts.astype(jnp.bfloat16))
    return jnp.sum(rounded.astype(jnp.float32), axis=0)


def expert_pass(operands):
    rows_mixed, rows_grad, weight_in, weight_out = operands
    pre_act = jnp.dot(rows_mixed, weight_in, preferred_element_type=jnp.float32)
    sigma_pre = jax.nn.sigmoid(pre_act)
    hidden = (pre_act * sigma_pre).astype(jnp.bfloat16)
    back_hidden = jnp.dot(rows_grad, weight_out.T, preferred_element_type=jnp.float32)
    slope = (back_hidden * sigma_pre * (1.0 + pre_act * (1.0 - sigma_pre))).astype(jnp.bfloat16)
    grad_in = jnp.dot(rows_mixed.T, slope, preferred_element_type=jnp.float32).astype(jnp.bfloat16)
    grad_out = jnp.dot(hidden.T, rows_grad, preferred_element_type=jnp.float32).astype(jnp.bfloat16)
    row_count = hidden.shape[0]
    block = FF // N_EXPERT
    hidden_split = hidden.reshape(row_count, N_EXPERT, block)
    slope_split = slope.reshape(row_count, N_EXPERT, block)
    out_split = weight_out.reshape(N_EXPERT, block, D)
    in_split = weight_in.reshape(D, N_EXPERT, block)
    expert_out = shard_sums(hidden_split, out_split, "rkh,khd->krd")
    grad_mixed = shard_sums(slope_split, in_split, "rkh,dkh->krd")
    return expert_out, grad_mixed, grad_in, grad_out


def reference(tokens, cotangent, group_of, mixer, w_in, w_out):
    ranking = jnp.argsort(group_of, axis=0, stable=True).astype(jnp.int32)
    picked = ranking[:, :, None]
    group_count = SEQS // GROUP
    grouped_tok = jnp.take_along_axis(tokens, picked, axis=0).astype(jnp.float32).reshape(group_count, GROUP, POSITIONS, D)
    grouped_cot = jnp.take_along_axis(cotangent, picked, axis=0).astype(jnp.float32).reshape(group_count, GROUP, POSITIONS, D)
    mixer_wide = mixer.astype(jnp.float32)
    logits = jnp.einsum("qgpd,de->qgpe", grouped_tok, mixer_wide)
    scaled = jnp.tanh(logits / soft_cap)
    exponent = jnp.exp(soft_cap * scaled)
    weights = exponent / jnp.sum(exponent, axis=1, keepdims=True)
    mixed = jnp.einsum("qgpe,qgpd->eqpd", weights, grouped_tok).astype(jnp.bfloat16)
    dmixed = jnp.einsum("qgpe,qgpd->eqpd", weights, grouped_cot).astype(jnp.bfloat16)
    rows_mixed = mixed.reshape(EXPERTS, group_count * POSITIONS, D)
    rows_grad = dmixed.reshape(EXPERTS, group_count * POSITIONS, D)
    expert_out, grad_mixed, grad_in, grad_out = lax.map(expert_pass, (rows_mixed, rows_grad, w_in, w_out))
    expert_out = expert_out.reshape(EXPERTS, group_count, POSITIONS, D)
    grad_mixed = grad_mixed.reshape(EXPERTS, group_count, POSITIONS, D)
    d_weights = jnp.einsum("qgpd,eqpd->qgpe", grouped_cot, expert_out) + jnp.einsum("qgpd,eqpd->qgpe", grouped_tok, grad_mixed)
    column_sum = jnp.sum(weights * d_weights, axis=1, keepdims=True)
    d_logits = weights * (d_weights - column_sum) * (1.0 - scaled * scaled)
    grad_group = jnp.einsum("qgpe,eqpd->qgpd", weights, grad_mixed) + jnp.einsum("qgpe,de->qgpd", d_logits, mixer_wide)
    grad_sorted = grad_group.astype(jnp.bfloat16).reshape(SEQS, POSITIONS, D)
    inverse = jnp.argsort(ranking, axis=0).astype(jnp.int32)
    grad_tokens = jnp.take_along_axis(grad_sorted, inverse[:, :, None], axis=0)
    grad_mixer = jnp.einsum("qgpd,qgpe->de", grouped_tok, d_logits)
    return grad_tokens, grad_mixer, grad_in, grad_out
```

```python
import jax
import jax.numpy as jnp
from jax import lax
from jax.sharding import Mesh
from jax.sharding import PartitionSpec as P

soft_cap = 15.0
f32 = jnp.float32
bf16 = jnp.bfloat16

axes = ("yh", "x", "core", "z", "b")
sizes = (2, 4, 2, 4, 2)
owners = ("yh", "x", "core")
same_core = ("yh", "x", "z", "b")
swap = [(0, 1), (1, 0)]


def mm(left, right, contract=((1,), (0,))):
    return lax.dot_general(left, right, (contract, ((), ())), preferred_element_type=f32)


def exchange(array, names):
    return lax.all_to_all(array, names, split_axis=0, concat_axis=0, tiled=True)


def split_high_low(value):
    high = lax.reduce_precision(value, 8, 7)
    return high.astype(bf16), (value - high).astype(bf16)


def weight_round(step):
    return [
        (s * 4 + z, (z // 2) * 4 + 2 * s + (z + step) % 2) for s in range(2) for z in range(4)
    ]


def back_round(step):
    return [(b, a) for a, b in weight_round(step)]


def shards(tokens, cotangent, group_of, mixer, w_in, w_out):
    seqs, positions, width = tokens.shape
    rows = seqs * positions
    core = lax.axis_index("core")
    first = core == 0
    even = lax.axis_index("z") % 2 == 0
    half = width // 2

    def pick(flag, one, other):
        return jnp.where(flag, one, other)

    home = group_of % 16
    earlier = jnp.arange(seqs)[:, None] > jnp.arange(seqs)[None, :]
    same = (home[:, None, :] == home[None, :, :]) & earlier[:, :, None]
    member = jnp.sum(same.astype(jnp.int32), axis=1)
    place = home * 8 + jnp.arange(positions, dtype=jnp.int32)[None, :] * 2 + member
    hot = (place.reshape(1, rows) == jnp.arange(rows, dtype=jnp.int32)[:, None]).astype(bf16)
    tok = mm(hot, tokens.reshape(rows, width)).astype(bf16).reshape(8, 1, 16, width)
    cot = mm(hot, cotangent.reshape(rows, width)).astype(bf16).reshape(8, 1, 16, width)
    sent = jnp.concatenate([tok, cot], axis=1).reshape(16, 16, width)
    held = exchange(sent, owners).reshape(256, width)

    weights_in, weights_out = [], []
    for step in range(2):
        flag = even if step == 0 else jnp.logical_not(even)
        weights_in.append(
            lax.ppermute(pick(flag, w_in[0], w_in[1]), ("core", "z"), weight_round(step))
        )
        weights_out.append(
            lax.ppermute(pick(flag, w_out[0], w_out[1]), ("core", "z"), weight_round(step))
        )

    mixer_t = mixer.T
    logits = mm(mixer_t, held, ((1,), (1,)))
    logits = pick(first, logits, lax.ppermute(logits, "core", swap))
    scaled = jnp.tanh(logits / soft_cap)
    exponent = jnp.exp(soft_cap * scaled)
    column = jnp.arange(256, dtype=jnp.int32) // 2 % 8
    mask = (column[None, :] == jnp.arange(8, dtype=jnp.int32)[:, None]).astype(f32)
    spread = exponent[:, None, :] * mask[None]
    spread = spread / jnp.sum(spread, axis=2, keepdims=True)
    spread_high, spread_low = split_high_low(spread)
    mix = mm(spread_high.reshape(256, 256), held) + mm(spread_low.reshape(256, 256), held)
    mix = mix.astype(bf16).reshape(32, 1, 8, width)
    mix = jnp.broadcast_to(mix, (32, 2, 8, width)).reshape(64, 8, width)
    own_rows = exchange(mix, same_core).reshape(512, width)
    other_rows = lax.ppermute(own_rows, "core", swap)
    mixed = pick(first, own_rows, other_rows)
    dmixed = pick(first, other_rows, own_rows)

    expert_in = jnp.concatenate(weights_in, axis=1)
    expert_out = jnp.concatenate(weights_out, axis=0)
    pre_act = mm(mixed, expert_in)
    sigma_pre = jax.nn.sigmoid(pre_act)
    hidden = (pre_act * sigma_pre).astype(bf16)
    back_hidden = mm(dmixed, expert_out, ((1,), (1,)))
    slope = (back_hidden * sigma_pre * (1.0 + pre_act * (1.0 - sigma_pre))).astype(bf16)
    part_out = mm(hidden, expert_out).astype(bf16)
    part_grad = mm(slope, expert_in, ((1,), (1,))).astype(bf16)
    kept = pick(first, part_grad, part_out)
    given = lax.ppermute(pick(first, part_out, part_grad), "core", swap)
    part = (kept.astype(f32) + given.astype(f32)).astype(bf16)
    back = exchange(part.reshape(64, 8, width), same_core).reshape(512, width)

    grads_in, grads_out = [], []
    for step in range(2):
        block = slice(256 * step, 256 * step + 256)
        grads_in.append(
            lax.ppermute(
                mm(mixed, slope[:, block], ((0,), (0,))).astype(bf16),
                ("core", "z"),
                back_round(step),
            )
        )
        grads_out.append(
            lax.ppermute(
                mm(hidden[:, block], dmixed, ((0,), (0,))).astype(bf16),
                ("core", "z"),
                back_round(step),
            )
        )
    grad_in = jnp.stack(
        [pick(even, grads_in[0], grads_in[1]), pick(even, grads_in[1], grads_in[0])]
    )
    grad_out = jnp.stack(
        [pick(even, grads_out[0], grads_out[1]), pick(even, grads_out[1], grads_out[0])]
    )

    back_half = pick(first, back[:, :half], lax.ppermute(back[:, half:], "core", swap))
    dots = mm(back, held, ((1,), (1,))).reshape(32, 2, 8, 256)
    dots = jnp.sum(dots * mask[None, None], axis=(1, 2))
    d_weights = dots + lax.ppermute(dots, "core", swap)
    weights = jnp.sum(spread, axis=1)
    column_sum = jnp.sum((weights * d_weights)[:, None, :] * mask[None], axis=2, keepdims=True)
    column_sum = jnp.sum(column_sum * mask[None], axis=1)
    d_logits = weights * (d_weights - column_sum) * (1.0 - scaled * scaled)
    d_high, d_low = split_high_low(d_logits)

    both_high = jnp.broadcast_to(spread_high[:, None], (32, 2, 8, 256)).reshape(512, 256)
    both_low = jnp.broadcast_to(spread_low[:, None], (32, 2, 8, 256)).reshape(512, 256)
    mixer_half = pick(first, mixer_t[:, :half], mixer_t[:, half:])
    down = ((0,), (0,))
    grad_rows = (
        mm(both_high, back_half, down)
        + mm(both_low, back_half, down)
        + mm(d_high, mixer_half, down)
        + mm(d_low, mixer_half, down)
    )
    grad_rows = exchange(grad_rows.astype(bf16).reshape(16, 16, half), owners)
    grad_rows = grad_rows.reshape(8, 2, 16, half)
    grad_tokens = jnp.concatenate(
        [mm(hot, grad_rows[:, side].reshape(rows, half), down).astype(bf16) for side in range(2)],
        axis=1,
    ).reshape(seqs, positions, width)

    mixer_part = mm(d_high, held) + mm(d_low, held)
    mixer_part = pick(first, mixer_part, jnp.zeros_like(mixer_part))
    pieces = exchange(mixer_part.reshape(128, 8, 128), axes)
    total = jnp.sum(pieces, axis=0, keepdims=True)
    whole = exchange(jnp.broadcast_to(total, (128, 8, 128)), axes)
    grad_mixer = whole.reshape(32, width).T
    return (grad_tokens, grad_mixer, grad_in, grad_out)


def solution(mesh):
    fine = Mesh(mesh.devices.reshape(sizes), axes)
    dp, expert = ("yh", "x", "core"), ("z", "b")
    every = dp + expert
    return jax.shard_map(
        shards,
        mesh=fine,
        in_specs=(
            P(every, None, None),
            P(every, None, None),
            P(every, None),
            P(),
            P(dp, None, expert),
            P(dp, expert, None),
        ),
        out_specs=(
            P(every, None, None),
            P(),
            P(dp, None, expert),
            P(dp, expert, None),
        ),
        check_vma=False,
    )
```

```python
import functools

import jax
import jax.numpy as jnp
from jax import lax
from jax.experimental import pallas as pl
from jax.experimental.pallas import tpu as pltpu
from jax.sharding import Mesh
from jax.sharding import PartitionSpec as P

soft_cap = 15.0
f32 = jnp.float32
bf16 = jnp.bfloat16

axes = ("yh", "x", "core", "z", "b")
sizes = (2, 4, 2, 4, 2)
owners = ("yh", "x", "core")
planes = ("yh", "x", "z")
column = ("core", "z")
swap = [(0, 1), (1, 0)]
NN = ((1,), (0,))
NT = ((1,), (1,))
TN = ((0,), (0,))

any_spec = pl.BlockSpec(memory_space=pl.ANY)
vmem_spec = pl.BlockSpec(memory_space=pltpu.VMEM)
smem_spec = pl.BlockSpec(memory_space=pltpu.SMEM)
roomy = pltpu.CompilerParams(vmem_limit_bytes=48 * 1024 * 1024)


def mm(left, right, contract=NN):
    return lax.dot_general(left, right, (contract, ((), ())), preferred_element_type=f32)


def exchange(array, names):
    return lax.all_to_all(array, names, split_axis=0, concat_axis=0, tiled=True)


def split_high_low(value):
    high = lax.reduce_precision(value, 8, 7)
    return high.astype(bf16), (value - high).astype(bf16)


def weight_round(step):
    pairs = []
    for s in range(2):
        for z in range(4):
            q = (z + step) % 4
            pairs.append((s * 4 + z, (q % 2) * 4 + 2 * s + q // 2))
    return pairs


def back_round(step):
    return [(b, a) for a, b in weight_round(step)]


def piece_copies(piece, w_in, w_out, packed, sem, back):
    expert = piece // 2
    if piece % 2 == 1:
        pairs = [(w_out.at[expert], packed)]
    else:
        pairs = [
            (
                w_in.at[expert, pl.ds(256 * a, 256), :],
                packed.at[:, pl.ds(256 * a, 256)],
            )
            for a in range(16)
        ]
    for one, two in pairs:
        source, target = (two, one) if back else (one, two)
        pltpu.make_async_copy(source, target, sem).start()


def pack_body(z_ref, w_in, w_out, p0, p1, p2, p3, sems):
    packed = (p0, p1, p2, p3)
    for step in range(4):
        for piece in range(4):
            @pl.when((z_ref[0] + step) % 4 == piece)
            def _():
                piece_copies(piece, w_in, w_out, packed[step], sems.at[step], False)
    for step in range(4):
        pltpu.make_async_copy(w_out.at[0], packed[step], sems.at[step]).wait()


def pack(z, w_in, w_out):
    shape = jax.ShapeDtypeStruct((256, 4096), bf16)
    return pl.pallas_call(
        pack_body,
        out_shape=(shape,) * 4,
        in_specs=[smem_spec, any_spec, any_spec],
        out_specs=(any_spec,) * 4,
        scratch_shapes=[pltpu.SemaphoreType.DMA((4,))],
        cost_estimate=pl.CostEstimate(flops=0, bytes_accessed=16 << 20, transcendentals=0),
    )(z, w_in, w_out)


def unpack_body(z_ref, p0, p1, p2, p3, w_in, w_out, sems):
    packed = (p0, p1, p2, p3)
    for step in range(4):
        for piece in range(4):
            @pl.when((z_ref[0] + step) % 4 == piece)
            def _():
                piece_copies(piece, w_in, w_out, packed[step], sems.at[step], True)
    for step in range(4):
        pltpu.make_async_copy(packed[step], w_out.at[0], sems.at[step]).wait()


def unpack(z, pieces):
    return pl.pallas_call(
        unpack_body,
        out_shape=(
            jax.ShapeDtypeStruct((2, 4096, 256), bf16),
            jax.ShapeDtypeStruct((2, 256, 4096), bf16),
        ),
        in_specs=[smem_spec] + [any_spec] * 4,
        out_specs=(any_spec, any_spec),
        scratch_shapes=[pltpu.SemaphoreType.DMA((4,))],
        cost_estimate=pl.CostEstimate(flops=0, bytes_accessed=16 << 20, transcendentals=0),
    )(z, *pieces)


def load_weights(core, weights, held, sems):
    for slot in range(4):
        @pl.when(core == 0)
        def _():
            pltpu.make_async_copy(weights[slot], held.at[slot], sems.at[slot]).start()

        @pl.when(core == 1)
        def _():
            pltpu.make_async_copy(weights[(slot + 1) % 4], held.at[slot], sems.at[slot]).start()


def wait_weights(slot, weights, held, sems):
    pltpu.make_async_copy(weights[0], held.at[slot], sems.at[slot]).wait()


def up_body(core_ref, r00, r01, r10, r11, w0, w1, w2, w3, pre_ref, send_ref, held, sems):
    core = core_ref[0]
    weights = (w0, w1, w2, w3)
    load_weights(core, weights, held, sems)

    def slot_step(slot, carry):
        wait_weights(slot, weights, held, sems)
        for block, (low, high) in enumerate(((r00, r01), (r10, r11))):
            here = pl.ds(256 * block, 256)

            @pl.when(core == 0)
            def _():
                total = jnp.zeros((256, 256), f32)
                for a in range(16):
                    rows = (low if a < 8 else high)[:, 256 * (a % 8) : 256 * (a % 8) + 256]
                    total += mm(rows, held[slot, :, 256 * a : 256 * a + 256])
                pre_ref[slot, here, :] = total
                send_ref[slot, here, :] = (total * jax.nn.sigmoid(total)).astype(bf16)

            @pl.when(core == 1)
            def _():
                total = mm(low[...], held[slot, :, :2048], NT) + mm(high[...], held[slot, :, 2048:], NT)
                send_ref[slot, here, :] = total.astype(bf16)

        return carry

    lax.fori_loop(0, 4, slot_step, 0)


def up(core, rows, weights):
    return pl.pallas_call(
        up_body,
        out_shape=(
            jax.ShapeDtypeStruct((4, 512, 256), f32),
            jax.ShapeDtypeStruct((4, 512, 256), bf16),
        ),
        in_specs=[smem_spec] + [vmem_spec] * 4 + [any_spec] * 4,
        out_specs=(vmem_spec, vmem_spec),
        scratch_shapes=[pltpu.VMEM((4, 256, 4096), bf16), pltpu.SemaphoreType.DMA((4,))],
        compiler_params=roomy,
        cost_estimate=pl.CostEstimate(flops=2 * 512 * 4096 * 1024, bytes_accessed=15 << 20, transcendentals=512 * 1024),
    )(core, *rows, *weights)


def down_body(core_ref, pre_ref, got_ref, w0, w1, w2, w3, o00, o01, o10, o11, q_ref, held, sems):
    core = core_ref[0]
    weights = (w0, w1, w2, w3)
    load_weights(core, weights, held, sems)

    @pl.when(core == 0)
    def _():
        for slot in range(4):
            pre_act = pre_ref[slot]
            sigma_pre = jax.nn.sigmoid(pre_act)
            slope = got_ref[slot].astype(f32) * sigma_pre * (1.0 + pre_act * (1.0 - sigma_pre))
            q_ref[slot] = slope.astype(bf16)

    @pl.when(core == 1)
    def _():
        q_ref[...] = got_ref[...]

    for slot in range(4):
        wait_weights(slot, weights, held, sems)
    for half, (own, other) in enumerate(((o00, o10), (o01, o11))):
        def part_step(a, carry):
            there = pl.ds(pl.multiple_of(256 * a + 2048 * half, 256), 256)
            here = pl.ds(pl.multiple_of(256 * a, 256), 256)
            for block, target in enumerate((own, other)):
                rows = pl.ds(256 * block, 256)

                @pl.when(core == 0)
                def _():
                    total = jnp.zeros((256, 256), f32)
                    for slot in range(4):
                        total += mm(q_ref[slot, rows, :], held[slot, :, there], NT)
                    target[:, here] = total.astype(bf16)

                @pl.when(core == 1)
                def _():
                    total = jnp.zeros((256, 256), f32)
                    for slot in range(4):
                        total += mm(q_ref[slot, rows, :], held[slot, :, there])
                    target[:, here] = total.astype(bf16)

            return carry

        lax.fori_loop(0, 8, part_step, 0)


def down(core, pre_act, got, weights):
    piece = jax.ShapeDtypeStruct((256, 2048), bf16)
    return pl.pallas_call(
        down_body,
        out_shape=(piece,) * 4 + (jax.ShapeDtypeStruct((4, 512, 256), bf16),),
        in_specs=[smem_spec] + [vmem_spec] * 2 + [any_spec] * 4,
        out_specs=(vmem_spec,) * 5,
        scratch_shapes=[pltpu.VMEM((4, 256, 4096), bf16), pltpu.SemaphoreType.DMA((4,))],
        compiler_params=roomy,
        cost_estimate=pl.CostEstimate(flops=2 * 512 * 4096 * 1024, bytes_accessed=16 << 20, transcendentals=512 * 1024),
    )(core, pre_act, got, *weights)


def grads_body(core_ref, r00, r01, r10, r11, q_ref, g0, g1, g2, g3, held, sems):
    core = core_ref[0]
    grads = (g0, g1, g2, g3)

    @pl.when(core == 0)
    def _():
        for half, (own, other) in enumerate(((r00, r10), (r01, r11))):
            def token_step(a, carry):
                here = pl.ds(pl.multiple_of(256 * a, 256), 256)
                there = pl.ds(pl.multiple_of(256 * a + 2048 * half, 256), 256)
                for slot in range(4):
                    total = mm(own[:, here], q_ref[slot, :256, :], TN)
                    total += mm(other[:, here], q_ref[slot, 256:, :], TN)
                    held[slot, :, there] = total.astype(bf16)
                return carry

            lax.fori_loop(0, 8, token_step, 0)

    @pl.when(core == 1)
    def _():
        for half, (own, other) in enumerate(((r00, r10), (r01, r11))):
            def grad_step(a, carry):
                here = pl.ds(pl.multiple_of(256 * a, 256), 256)
                there = pl.ds(pl.multiple_of(256 * a + 2048 * half, 256), 256)
                for slot in range(4):
                    total = mm(q_ref[slot, :256, :], own[:, here], TN)
                    total += mm(q_ref[slot, 256:, :], other[:, here], TN)
                    held[slot, :, there] = total.astype(bf16)
                return carry

            lax.fori_loop(0, 8, grad_step, 0)

    for slot in range(4):
        @pl.when(core == 0)
        def _():
            pltpu.make_async_copy(held.at[slot], grads[slot], sems.at[slot]).start()

        @pl.when(core == 1)
        def _():
            pltpu.make_async_copy(held.at[slot], grads[(slot + 1) % 4], sems.at[slot]).start()

    for slot in range(4):
        pltpu.make_async_copy(held.at[slot], grads[0], sems.at[slot]).wait()


def weight_grads(core, rows, units):
    shape = jax.ShapeDtypeStruct((256, 4096), bf16)
    return pl.pallas_call(
        grads_body,
        out_shape=(shape,) * 4,
        in_specs=[smem_spec] + [vmem_spec] * 5,
        out_specs=(any_spec,) * 4,
        scratch_shapes=[pltpu.VMEM((4, 256, 4096), bf16), pltpu.SemaphoreType.DMA((4,))],
        compiler_params=roomy,
        cost_estimate=pl.CostEstimate(flops=2 * 512 * 4096 * 1024, bytes_accessed=13 << 20, transcendentals=0),
    )(core, *rows, units)


def shards(tokens, cotangent, group_of, mixer, w_in, w_out):
    seqs, positions, width = tokens.shape
    rows = seqs * positions
    core = lax.axis_index("core")
    first = core == 0
    half = width // 2
    core_at = core.astype(jnp.int32).reshape(1)
    z_at = lax.axis_index("z").astype(jnp.int32).reshape(1)
    tie = lax.optimization_barrier

    weights = [
        lax.ppermute(piece, column, weight_round(step))
        for step, piece in enumerate(pack(z_at, w_in, w_out))
    ]

    home = group_of % 16
    earlier = jnp.arange(seqs)[:, None] > jnp.arange(seqs)[None, :]
    same = (home[:, None, :] == home[None, :, :]) & earlier[:, :, None]
    member = jnp.sum(same.astype(jnp.int32), axis=1)
    place = home * 8 + jnp.arange(positions, dtype=jnp.int32)[None, :] * 2 + member
    hot = (place.reshape(1, rows) == jnp.arange(rows, dtype=jnp.int32)[:, None]).astype(bf16)
    tok = mm(hot, tokens.reshape(rows, width)).astype(bf16).reshape(8, 1, 16, width)
    cot = mm(hot, cotangent.reshape(rows, width)).astype(bf16).reshape(8, 1, 16, width)
    sent = jnp.concatenate([tok, cot], axis=1).reshape(16, 16, width)
    held = exchange(sent, owners).reshape(256, width)

    mixer_t = mixer.T
    logits = mm(mixer_t, held, NT)
    logits = jnp.where(first, logits, lax.ppermute(logits, "core", swap))
    scaled = jnp.tanh(logits / soft_cap)
    exponent = jnp.exp(soft_cap * scaled)
    column_of = jnp.arange(256, dtype=jnp.int32) // 2 % 8
    mask = (column_of[None, :] == jnp.arange(8, dtype=jnp.int32)[:, None]).astype(f32)
    spread = exponent[:, None, :] * mask[None]
    spread = spread / jnp.sum(spread, axis=2, keepdims=True)
    spread_high, spread_low = split_high_low(spread)
    flat_high, flat_low = spread_high.reshape(256, 256), spread_low.reshape(256, 256)

    def mix(side):
        part = held[:, half * side : half * side + half]
        return (mm(flat_high, part) + mm(flat_low, part)).astype(bf16).reshape(32, 8, half)

    mix_0, weights[0], weights[1] = tie((mix(0), weights[0], weights[1]))
    own_0 = exchange(mix_0, planes).reshape(256, half)
    other_0 = lax.ppermute(own_0, "b", swap)
    own_1 = exchange(mix(1), planes).reshape(256, half)
    own_1, weights[2], weights[3] = tie((own_1, weights[2], weights[3]))
    other_1 = lax.ppermute(own_1, "b", swap)
    expert_rows = (own_0, own_1, other_0, other_1)

    pre_act, given = up(core_at, expert_rows, weights)
    got = lax.ppermute(given, "core", swap)
    part_0, part_1, away_0, away_1, units = down(core_at, pre_act, got, weights)

    def home_sum(part, away):
        come = lax.ppermute(away, "b", swap)
        total = (part.astype(f32) + come.astype(f32)).astype(bf16)
        return exchange(total.reshape(32, 8, half), planes).reshape(256, half)

    back_0 = home_sum(part_0, away_0)
    back_1 = home_sum(part_1, away_1)

    grads = [
        lax.ppermute(piece, column, back_round(step))
        for step, piece in enumerate(weight_grads(core_at, expert_rows, units))
    ]

    back_half = jnp.where(first, back_1, lax.ppermute(back_0, "core", swap))
    dots = mm(back_0, held[:, :half], NT) + mm(back_1, held[:, half:], NT)
    dots = jnp.sum(dots.reshape(32, 8, 256) * mask[None], axis=1)
    d_weights = dots + lax.ppermute(dots, "core", swap)
    mixing = jnp.sum(spread, axis=1)
    column_sum = jnp.sum((mixing * d_weights)[:, None, :] * mask[None], axis=2, keepdims=True)
    column_sum = jnp.sum(column_sum * mask[None], axis=1)
    d_logits = mixing * (d_weights - column_sum) * (1.0 - scaled * scaled)
    d_high, d_low = split_high_low(d_logits)

    mixer_part = mm(d_high, held) + mm(d_low, held)
    mixer_part = jnp.where(first, mixer_part, jnp.zeros_like(mixer_part))
    pieces = exchange(mixer_part.reshape(128, 8, 128), axes)
    total = jnp.sum(pieces, axis=0, keepdims=True)

    mixer_half = jnp.where(first, mixer_t[:, half:], mixer_t[:, :half])
    grad_rows = (
        mm(flat_high, back_half, TN)
        + mm(flat_low, back_half, TN)
        + mm(d_high, mixer_half, TN)
        + mm(d_low, mixer_half, TN)
    )
    grad_rows = exchange(grad_rows.astype(bf16).reshape(16, 16, half), owners)
    grad_rows, grads[0], grads[1], grads[2], grads[3] = tie((grad_rows, *grads))
    grad_in, grad_out = unpack(z_at, grads)
    grad_rows = grad_rows.reshape(8, 2, 16, half)
    grad_tokens = jnp.concatenate(
        [mm(hot, grad_rows[:, 1 - side].reshape(rows, half), TN).astype(bf16) for side in range(2)],
        axis=1,
    ).reshape(seqs, positions, width)

    whole = exchange(jnp.broadcast_to(total, (128, 8, 128)), axes)
    grad_mixer = whole.reshape(32, width).T
    return (grad_tokens, grad_mixer, grad_in, grad_out)


def solution(mesh):
    fine = Mesh(mesh.devices.reshape(sizes), axes)
    dp, expert = ("yh", "x", "core"), ("z", "b")
    every = dp + expert
    return jax.shard_map(
        shards,
        mesh=fine,
        in_specs=(
            P(every, None, None),
            P(every, None, None),
            P(every, None),
            P(),
            P(dp, None, expert),
            P(dp, expert, None),
        ),
        out_specs=(
            P(every, None, None),
            P(),
            P(dp, None, expert),
            P(dp, expert, None),
        ),
        check_vma=False,
    )
```

```python
import functools

import jax
import jax.numpy as jnp
from jax import lax
from jax.experimental import pallas as pl
from jax.experimental.pallas import tpu as pltpu
from jax.sharding import Mesh
from jax.sharding import PartitionSpec as P

soft_cap = 15.0
f32 = jnp.float32
bf16 = jnp.bfloat16

axes = ("yh", "x", "core", "z", "b")
sizes = (2, 4, 2, 4, 2)
owners = ("yh", "x", "core")
near = ("yh", "x", "b")
column = ("core", "z")
swap = [(0, 1), (1, 0)]
NN = ((1,), (0,))
NT = ((1,), (1,))
TN = ((0,), (0,))

any_spec = pl.BlockSpec(memory_space=pl.ANY)
vmem_spec = pl.BlockSpec(memory_space=pltpu.VMEM)
smem_spec = pl.BlockSpec(memory_space=pltpu.SMEM)
roomy = pltpu.CompilerParams(vmem_limit_bytes=48 * 1024 * 1024)


def mm(left, right, contract=NN):
    return lax.dot_general(left, right, (contract, ((), ())), preferred_element_type=f32)


def exchange(array, names):
    return lax.all_to_all(array, names, split_axis=0, concat_axis=0, tiled=True)


def split_high_low(value):
    high = lax.reduce_precision(value, 8, 7)
    return high.astype(bf16), (value - high).astype(bf16)


def piece_of(step, z):
    return ((z + 1 + step // 2) % 2) * 2 + (step + z // 2) % 2


def weight_round(step):
    pairs = []
    for s in range(2):
        for z in range(4):
            q = piece_of(step, z)
            pairs.append((s * 4 + z, (q % 2) * 4 + 2 * s + q // 2))
    return [(a, b) for a, b in pairs if a != b]


def own_step(core, z):
    table = [-1] * 8
    for step in range(4):
        sending = [a for a, _ in weight_round(step)]
        for at in range(8):
            if at not in sending:
                table[at] = step
    return jnp.array(table, jnp.int32)[core * 4 + z]


def back_round(step):
    return [(b, a) for a, b in weight_round(step)]


def piece_copies(piece, w_in, w_out, packed):
    expert = piece // 2
    if piece % 2 == 1:
        return [(w_out.at[expert], packed)]
    return [
        (w_in.at[expert, pl.ds(256 * a, 256), :], packed.at[:, pl.ds(256 * a, 256)])
        for a in range(16)
    ]


def sort_body(
    at_ref, place_ref, tokens, cotangent, w_in, w_out, sent, p0, p1, p2, p3, held, taken, put
):
    packed = (p0, p1, p2, p3)
    for step in range(4):
        for piece in range(4):
            @pl.when(at_ref[2 + step] == piece)
            def _():
                for source, target in piece_copies(piece, w_in, w_out, held.at[step]):
                    pltpu.make_async_copy(source, target, taken.at[step]).start()
    rows = tokens.shape[0]
    hot = (lax.broadcasted_iota(jnp.int32, (rows, rows), 0) == place_ref[...]).astype(bf16)
    for start in range(0, tokens.shape[1], 512):
        here = pl.ds(start, 512)
        sent[:, 0, :, here] = mm(hot, tokens[:, here]).astype(bf16).reshape(8, 16, 512)
        sent[:, 1, :, here] = mm(hot, cotangent[:, here]).astype(bf16).reshape(8, 16, 512)
    for step in range(4):
        pltpu.make_async_copy(w_out.at[0], held.at[step], taken.at[step]).wait()
        pltpu.make_async_copy(held.at[step], packed[step], put.at[step]).start()
    for step in range(4):
        pltpu.make_async_copy(held.at[step], packed[step], put.at[step]).wait()


def sort_and_pack(at, place, tokens, cotangent, w_in, w_out):
    shape = jax.ShapeDtypeStruct((256, 4096), bf16)
    return pl.pallas_call(
        sort_body,
        out_shape=(jax.ShapeDtypeStruct((8, 2, 16, 4096), bf16),) + (shape,) * 4,
        in_specs=[smem_spec] + [vmem_spec] * 3 + [any_spec] * 2,
        out_specs=(vmem_spec,) + (any_spec,) * 4,
        scratch_shapes=[
            pltpu.VMEM((4, 256, 4096), bf16),
            pltpu.SemaphoreType.DMA((4,)),
            pltpu.SemaphoreType.DMA((4,)),
        ],
        compiler_params=roomy,
        cost_estimate=pl.CostEstimate(flops=0, bytes_accessed=20 << 20, transcendentals=0),
    )(at, place, tokens, cotangent, w_in, w_out)


def unpack_body(
    at_ref, p0, p1, p2, p3, q0, q1, q2, q3, w_in, w_out, held, taken, put
):
    come, made = (p0, p1, p2, p3), (q0, q1, q2, q3)
    for step in range(4):
        @pl.when(at_ref[1] == step)
        def _():
            pltpu.make_async_copy(made[step], held.at[step], taken.at[step]).start()

        @pl.when(at_ref[1] != step)
        def _():
            pltpu.make_async_copy(come[step], held.at[step], taken.at[step]).start()
    for step in range(4):
        pltpu.make_async_copy(come[step], held.at[step], taken.at[step]).wait()
        for piece in range(4):
            @pl.when(at_ref[2 + step] == piece)
            def _():
                for target, source in piece_copies(piece, w_in, w_out, held.at[step]):
                    pltpu.make_async_copy(source, target, put.at[step]).start()
    for step in range(4):
        pltpu.make_async_copy(held.at[step], w_out.at[0], put.at[step]).wait()


def unpack(at, come, made):
    return pl.pallas_call(
        unpack_body,
        out_shape=(
            jax.ShapeDtypeStruct((2, 4096, 256), bf16),
            jax.ShapeDtypeStruct((2, 256, 4096), bf16),
        ),
        in_specs=[smem_spec] + [any_spec] * 8,
        out_specs=(any_spec, any_spec),
        scratch_shapes=[
            pltpu.VMEM((4, 256, 4096), bf16),
            pltpu.SemaphoreType.DMA((4,)),
            pltpu.SemaphoreType.DMA((4,)),
        ],
        compiler_params=roomy,
        cost_estimate=pl.CostEstimate(flops=0, bytes_accessed=16 << 20, transcendentals=0),
    )(at, *come, *made)


def load_weights(at_ref, weights, packed, tall, wide, sems):
    def load_tall(slot, array):
        for a in range(16):
            block = pl.ds(256 * a, 256)
            target = tall.at[block, pl.ds(256 * slot, 256)]
            pltpu.make_async_copy(array.at[:, block], target, sems.at[slot]).start()

    def load_wide(slot, array):
        target = wide.at[pl.ds(256 * slot, 256), :]
        pltpu.make_async_copy(array, target, sems.at[slot]).start()

    core, own = at_ref[0], at_ref[1]
    for slot in range(4):
        for here, step, load in ((0, slot, load_tall), (1, slot ^ 1, load_wide)):
            @pl.when((core == here) & (own == step))
            def _():
                load(slot, packed[step])

            @pl.when((core == here) & (own != step))
            def _():
                load(slot, weights[step])


def wait_weights(slot, weights, wide, sems):
    pltpu.make_async_copy(weights[0], wide.at[pl.ds(256 * slot, 256), :], sems.at[slot]).wait()


def up_body(
    at_ref, rows_in, w0, w1, w2, w3, p0, p1, p2, p3,
    pre_ref, send_ref, rows, tall, wide, row_sem, sems,
):
    core = at_ref[0]
    weights = (w0, w1, w2, w3)
    pltpu.make_async_copy(rows_in, rows, row_sem).start()
    load_weights(at_ref, weights, (p0, p1, p2, p3), tall, wide, sems)
    pltpu.make_async_copy(rows_in, rows, row_sem).wait()

    @pl.when(core == 0)
    def _():
        for slot in range(4):
            wait_weights(slot, weights, wide, sems)
            here = slice(256 * slot, 256 * slot + 256)
            pre_act = mm(rows[...], tall[:, here])
            pre_ref[:, here] = pre_act
            send_ref[:, here] = (pre_act * jax.nn.sigmoid(pre_act)).astype(bf16)

    @pl.when(core == 1)
    def _():
        for slot in range(4):
            wait_weights(slot, weights, wide, sems)
            here = slice(256 * slot, 256 * slot + 256)
            send_ref[:, here] = mm(rows[...], wide[here, :], NT).astype(bf16)


def up(at, rows, weights, packed):
    return pl.pallas_call(
        up_body,
        out_shape=(
            jax.ShapeDtypeStruct((512, 1024), f32),
            jax.ShapeDtypeStruct((512, 1024), bf16),
        ),
        in_specs=[smem_spec] + [any_spec] * 9,
        out_specs=(vmem_spec, vmem_spec),
        scratch_shapes=[
            pltpu.VMEM((512, 4096), bf16),
            pltpu.VMEM((4096, 1024), bf16),
            pltpu.VMEM((1024, 4096), bf16),
            pltpu.SemaphoreType.DMA,
            pltpu.SemaphoreType.DMA((4,)),
        ],
        compiler_params=roomy,
        cost_estimate=pl.CostEstimate(
            flops=2 * 512 * 4096 * 1024, bytes_accessed=15 << 20, transcendentals=512 * 1024
        ),
    )(at, rows, *weights, *packed)


def down_body(
    at_ref, pre_ref, got_ref, w0, w1, w2, w3, p0, p1, p2, p3,
    part_ref, q_ref, tall, wide, sems,
):
    core = at_ref[0]
    weights = (w0, w1, w2, w3)
    load_weights(at_ref, weights, (p0, p1, p2, p3), tall, wide, sems)

    @pl.when(core == 0)
    def _():
        for slot in range(4):
            here = slice(256 * slot, 256 * slot + 256)
            pre_act = pre_ref[:, here]
            sigma_pre = jax.nn.sigmoid(pre_act)
            slope = got_ref[:, here].astype(f32) * sigma_pre * (1.0 + pre_act * (1.0 - sigma_pre))
            q_ref[:, here] = slope.astype(bf16)

    @pl.when(core == 1)
    def _():
        q_ref[...] = got_ref[...]

    for slot in range(4):
        wait_weights(slot, weights, wide, sems)

    @pl.when(core == 0)
    def _():
        for index in range(8):
            here = slice(512 * index, 512 * index + 512)
            part_ref[:, here] = mm(q_ref[...], tall[here, :], NT).astype(bf16)

    @pl.when(core == 1)
    def _():
        for index in range(8):
            here = slice(512 * index, 512 * index + 512)
            part_ref[:, here] = mm(q_ref[...], wide[:, here]).astype(bf16)


def down(at, pre_act, got, weights, packed):
    return pl.pallas_call(
        down_body,
        out_shape=(
            jax.ShapeDtypeStruct((512, 4096), bf16),
            jax.ShapeDtypeStruct((512, 1024), bf16),
        ),
        in_specs=[smem_spec] + [vmem_spec] * 2 + [any_spec] * 8,
        out_specs=(vmem_spec,) * 2,
        scratch_shapes=[
            pltpu.VMEM((4096, 1024), bf16),
            pltpu.VMEM((1024, 4096), bf16),
            pltpu.SemaphoreType.DMA((4,)),
        ],
        compiler_params=roomy,
        cost_estimate=pl.CostEstimate(
            flops=2 * 512 * 4096 * 1024, bytes_accessed=16 << 20, transcendentals=512 * 1024
        ),
    )(at, pre_act, got, *weights, *packed)


def grads_body(at_ref, rows, q_ref, g0, g1, g2, g3, tall, wide, sems):
    core = at_ref[0]
    grads = (g0, g1, g2, g3)

    @pl.when(core == 0)
    def _():
        for slot in range(4):
            here = slice(256 * slot, 256 * slot + 256)
            tall[:, here] = mm(rows[...], q_ref[:, here], TN).astype(bf16)
            for a in range(16):
                block = pl.ds(256 * a, 256)
                source = tall.at[block, pl.ds(256 * slot, 256)]
                pltpu.make_async_copy(source, grads[slot].at[:, block], sems.at[slot]).start()

    @pl.when(core == 1)
    def _():
        for slot in range(4):
            here = slice(256 * slot, 256 * slot + 256)
            wide[here, :] = mm(q_ref[:, here], rows[...], TN).astype(bf16)
            source = wide.at[pl.ds(256 * slot, 256), :]
            pltpu.make_async_copy(source, grads[slot ^ 1], sems.at[slot]).start()

    for slot in range(4):
        pltpu.make_async_copy(wide.at[pl.ds(0, 256), :], grads[0], sems.at[slot]).wait()


def weight_grads(at, rows, units):
    shape = jax.ShapeDtypeStruct((256, 4096), bf16)
    return pl.pallas_call(
        grads_body,
        out_shape=(shape,) * 4,
        in_specs=[smem_spec] + [vmem_spec] * 2,
        out_specs=(any_spec,) * 4,
        scratch_shapes=[
            pltpu.VMEM((4096, 1024), bf16),
            pltpu.VMEM((1024, 4096), bf16),
            pltpu.SemaphoreType.DMA((4,)),
        ],
        compiler_params=roomy,
        cost_estimate=pl.CostEstimate(
            flops=2 * 512 * 4096 * 1024, bytes_accessed=13 << 20, transcendentals=0
        ),
    )(at, rows, units)


def shards(tokens, cotangent, group_of, mixer, w_in, w_out):
    seqs, positions, width = tokens.shape
    rows = seqs * positions
    core = lax.axis_index("core")
    first = core == 0
    half = width // 2
    plane = lax.axis_index("z")
    at = jnp.stack(
        [core, own_step(core, plane)] + [piece_of(step, plane) for step in range(4)]
    ).astype(jnp.int32)
    tie = lax.optimization_barrier

    home = group_of % 16
    earlier = jnp.arange(seqs)[:, None] > jnp.arange(seqs)[None, :]
    same = (home[:, None, :] == home[None, :, :]) & earlier[:, :, None]
    member = jnp.sum(same.astype(jnp.int32), axis=1)
    place = home * 8 + jnp.arange(positions, dtype=jnp.int32)[None, :] * 2 + member
    place = place.reshape(1, rows)
    sent, *packed = sort_and_pack(
        at, place, tokens.reshape(rows, width), cotangent.reshape(rows, width), w_in, w_out
    )
    hot = (place == jnp.arange(rows, dtype=jnp.int32)[:, None]).astype(bf16)
    held = exchange(sent.reshape(16, 16, width), owners).reshape(256, width)

    def send_weights(step, piece):
        return lax.ppermute(piece, column, weight_round(step))

    weights = [send_weights(0, packed[0]), send_weights(1, packed[1])]

    planes = [(plane + d) % 4 for d in range(4)]
    mixer_e = mixer.T.reshape(8, 4, width)
    mixer_t = jnp.concatenate(
        [lax.dynamic_index_in_dim(mixer_e, p, 1, keepdims=False) for p in planes], axis=0
    )
    logits = mm(mixer_t, held, NT)
    logits = jnp.where(first, logits, lax.ppermute(logits, "core", swap))
    scaled = jnp.tanh(logits / soft_cap)
    exponent = jnp.exp(soft_cap * scaled)
    column_of = jnp.arange(256, dtype=jnp.int32) // 2 % 8
    mask = (column_of[None, :] == jnp.arange(8, dtype=jnp.int32)[:, None]).astype(f32)
    spread = exponent[:, None, :] * mask[None]
    spread = spread / jnp.sum(spread, axis=2, keepdims=True)
    spread_high, spread_low = split_high_low(spread)
    flat_high, flat_low = spread_high.reshape(256, 256), spread_low.reshape(256, 256)

    def shift(by):
        return [(s, (s + by) % 4) for s in range(4)]

    mix = (mm(flat_high, held) + mm(flat_low, held)).astype(bf16)
    blocks = {}
    for d in (2, 1, 3, 0):
        block = mix[64 * d : 64 * d + 64]
        blocks[d] = lax.ppermute(block, "z", shift(d)) if d else block
    blocks[2], weights[0], weights[1], *later = tie(
        (blocks[2], weights[0], weights[1], *packed[2:])
    )
    weights += [send_weights(step + 2, piece) for step, piece in enumerate(later)]
    sent = jnp.stack([blocks[d].reshape(8, 8, width) for d in range(4)], axis=1)
    sent = jnp.broadcast_to(sent[:, None], (8, 2, 4, 8, width)).reshape(16, 32, width)
    expert_rows = exchange(sent, near).reshape(512, width)

    pre_act, given = up(at, expert_rows, weights, packed)
    got = lax.ppermute(given, "core", swap)
    part, units = down(at, pre_act, got, weights, packed)
    made = weight_grads(at, expert_rows, units)
    back = exchange(part.reshape(16, 32, width), near)

    def send_grads(step, piece):
        return lax.ppermute(piece, column, back_round(step))

    grads = [send_grads(step, made[step]) for step in range(2)]
    back, grads[0], grads[1] = tie((back, grads[0], grads[1]))
    back = jnp.sum(back.reshape(8, 2, 4, 8, width).astype(f32), axis=1).astype(bf16)
    blocks = {}
    for d in (2, 1, 3, 0):
        block = back[:, d].reshape(64, width)
        blocks[d] = lax.ppermute(block, "z", shift(-d)) if d else block
    blocks[2], *later = tie((blocks[2], *made[2:]))
    grads += [send_grads(step + 2, piece) for step, piece in enumerate(later)]
    dots, halves = [], []
    for d in range(4):
        block = blocks[d]
        dots.append(jnp.sum(mm(block, held, NT).reshape(8, 8, 256) * mask[None], axis=1))
        come = lax.ppermute(block[:, :half], "core", swap)
        halves.append(jnp.where(first, block[:, half:], come))
    dots = jnp.concatenate(dots, axis=0)
    back_half = jnp.concatenate(halves, axis=0)
    d_weights = dots + lax.ppermute(dots, "core", swap)
    mixing = jnp.sum(spread, axis=1)
    column_sum = jnp.sum((mixing * d_weights)[:, None, :] * mask[None], axis=2, keepdims=True)
    column_sum = jnp.sum(column_sum * mask[None], axis=1)
    d_logits = mixing * (d_weights - column_sum) * (1.0 - scaled * scaled)
    d_high, d_low = split_high_low(d_logits)

    mixer_half = jnp.where(first, mixer_t[:, half:], mixer_t[:, :half])
    grad_rows = (
        mm(flat_high, back_half, TN)
        + mm(flat_low, back_half, TN)
        + mm(d_high, mixer_half, TN)
        + mm(d_low, mixer_half, TN)
    )
    grad_rows = exchange(grad_rows.astype(bf16).reshape(16, 16, half), owners)

    here_yh, here_x = lax.axis_index("yh"), lax.axis_index("x")
    steps = jnp.arange(32, dtype=jnp.int32)
    far_x, far_yh, far_z = steps // 8, steps // 4 % 2, steps % 4
    at_x, at_yh = (here_x + far_x) % 4, (here_yh + far_yh) % 2
    take = far_z * 8 + at_yh * 4 + at_x
    turn = (take[:, None] == steps[None, :]).astype(bf16)
    part = mm(mm(turn, d_high).astype(bf16), held) + mm(mm(turn, d_low).astype(bf16), held)
    come = lax.ppermute(part[:, half:], "core", [(0, 1)])
    part = jnp.where(first, part[:, :half], come)
    low_b = lax.axis_index("b") == 0
    left, right = part[:, : half // 2], part[:, half // 2 :]
    part = jnp.where(low_b, left, right)
    part += lax.ppermute(jnp.where(low_b, right, left), "b", swap)
    part = part.reshape(4, 2, 4, half // 2)
    part = sum(
        [lax.ppermute(part[d], "x", shift(d)) for d in range(1, 4)], start=part[0]
    )
    part = part[0] + lax.ppermute(part[1], "yh", swap)
    part, grad_rows, grads[2], grads[3] = tie((part, grad_rows, grads[2], grads[3]))
    part = sum(
        [lax.ppermute(part[d : d + 1], "z", shift(d)) for d in range(1, 4)], start=part[:1]
    )
    part = jnp.concatenate(
        [part] + [lax.ppermute(part, "z", shift(-d)) for d in range(1, 4)], axis=0
    )
    part = jnp.stack([part, lax.ppermute(part, "yh", swap)], axis=0)
    part = jnp.stack([part] + [lax.ppermute(part, "x", shift(-d)) for d in range(1, 4)], axis=0)
    part = part.reshape(32, half // 2)
    come = lax.ppermute(part, "b", swap)
    part = jnp.concatenate([jnp.where(low_b, part, come), jnp.where(low_b, come, part)], axis=1)
    come = lax.ppermute(part, "core", swap)
    part = jnp.concatenate([jnp.where(first, part, come), jnp.where(first, come, part)], axis=1)
    expert_at = (at_yh * 4 + at_x) * 4 + (plane + far_z) % 4
    turn = (expert_at[:, None] == steps[None, :]).astype(f32)
    grad_mixer = lax.dot_general(
        part, turn, (TN, ((), ())), precision=lax.Precision.HIGHEST, preferred_element_type=f32
    )

    grad_in, grad_out = unpack(at, grads, made)
    grad_rows = grad_rows.reshape(8, 2, 16, half)
    grad_tokens = jnp.concatenate(
        [mm(hot, grad_rows[:, 1 - side].reshape(rows, half), TN).astype(bf16) for side in range(2)],
        axis=1,
    ).reshape(seqs, positions, width)
    return (grad_tokens, grad_mixer, grad_in, grad_out)


def solution(mesh):
    fine = Mesh(mesh.devices.reshape(sizes), axes)
    dp, expert = ("yh", "x", "core"), ("z", "b")
    every = dp + expert
    return jax.shard_map(
        shards,
        mesh=fine,
        in_specs=(
            P(every, None, None),
            P(every, None, None),
            P(every, None),
            P(),
            P(dp, None, expert),
            P(dp, expert, None),
        ),
        out_specs=(
            P(every, None, None),
            P(),
            P(dp, None, expert),
            P(dp, expert, None),
        ),
        check_vma=False,
    )
```

```python
import functools

import jax
import jax.numpy as jnp
from jax import lax
from jax.experimental import pallas as pl
from jax.experimental.pallas import tpu as pltpu
from jax.sharding import Mesh
from jax.sharding import PartitionSpec as P

soft_cap = 15.0
f32 = jnp.float32
bf16 = jnp.bfloat16

axes = ("yh", "x", "core", "z", "b")
sizes = (2, 4, 2, 4, 2)
owners = ("yh", "x", "core")
near = ("yh", "x", "b")
same_core = ("yh", "x", "z", "b")
column = ("core", "z")
swap = [(0, 1), (1, 0)]
NN = ((1,), (0,))
NT = ((1,), (1,))
TN = ((0,), (0,))

any_spec = pl.BlockSpec(memory_space=pl.ANY)
vmem_spec = pl.BlockSpec(memory_space=pltpu.VMEM)
smem_spec = pl.BlockSpec(memory_space=pltpu.SMEM)
roomy = pltpu.CompilerParams(vmem_limit_bytes=48 * 1024 * 1024)


def block_at(index, size):
    return pl.ds(pl.multiple_of(index * size, size), size)


def mm(left, right, contract=NN):
    return lax.dot_general(left, right, (contract, ((), ())), preferred_element_type=f32)


def exchange(array, names):
    return lax.all_to_all(array, names, split_axis=0, concat_axis=0, tiled=True)


def split_high_low(value):
    high = lax.reduce_precision(value, 8, 7)
    return high.astype(bf16), (value - high).astype(bf16)


def piece_of(step, z):
    return ((z + 1 + step // 2) % 2) * 2 + (step + z // 2) % 2


def weight_round(step):
    pairs = []
    for s in range(2):
        for z in range(4):
            q = piece_of(step, z)
            pairs.append((s * 4 + z, (q % 2) * 4 + 2 * s + q // 2))
    return [(a, b) for a, b in pairs if a != b]


def own_step(core, z):
    table = [-1] * 8
    for step in range(4):
        sending = [a for a, _ in weight_round(step)]
        for at in range(8):
            if at not in sending:
                table[at] = step
    return jnp.array(table, jnp.int32)[core * 4 + z]


def back_round(step):
    return [(b, a) for a, b in weight_round(step)]


def piece_copies(piece, w_in, w_out, packed):
    expert = piece // 2
    if piece % 2 == 1:
        return [(w_out.at[expert], packed)]
    return [
        (w_in.at[expert, pl.ds(256 * a, 256), :], packed.at[:, pl.ds(256 * a, 256)])
        for a in range(16)
    ]


def sort_body(
    at_ref, place_ref, tokens, cotangent, w_in, w_out, sent, p0, p1, p2, p3, held, taken, put
):
    packed = (p0, p1, p2, p3)
    for step in range(4):
        for piece in range(4):
            @pl.when(at_ref[2 + step] == piece)
            def _():
                for source, target in piece_copies(piece, w_in, w_out, held.at[step]):
                    pltpu.make_async_copy(source, target, taken.at[step]).start()
    rows = tokens.shape[0]
    hot = (lax.broadcasted_iota(jnp.int32, (rows, rows), 0) == place_ref[...]).astype(bf16)

    def step(index, carry):
        here = block_at(index, 512)
        sent[:, 0, :, here] = mm(hot, tokens[:, here]).astype(bf16).reshape(8, 16, 512)
        sent[:, 1, :, here] = mm(hot, cotangent[:, here]).astype(bf16).reshape(8, 16, 512)
        return carry

    lax.fori_loop(0, tokens.shape[1] // 512, step, 0)
    for step in range(4):
        pltpu.make_async_copy(w_out.at[0], held.at[step], taken.at[step]).wait()
        pltpu.make_async_copy(held.at[step], packed[step], put.at[step]).start()
    for step in range(4):
        pltpu.make_async_copy(held.at[step], packed[step], put.at[step]).wait()


def sort_and_pack(at, place, tokens, cotangent, w_in, w_out):
    shape = jax.ShapeDtypeStruct((256, 4096), bf16)
    return pl.pallas_call(
        sort_body,
        out_shape=(jax.ShapeDtypeStruct((8, 2, 16, 4096), bf16),) + (shape,) * 4,
        in_specs=[smem_spec] + [vmem_spec] * 3 + [any_spec] * 2,
        out_specs=(vmem_spec,) + (any_spec,) * 4,
        scratch_shapes=[
            pltpu.VMEM((4, 256, 4096), bf16),
            pltpu.SemaphoreType.DMA((4,)),
            pltpu.SemaphoreType.DMA((4,)),
        ],
        compiler_params=roomy,
        cost_estimate=pl.CostEstimate(flops=0, bytes_accessed=20 << 20, transcendentals=0),
    )(at, place, tokens, cotangent, w_in, w_out)


def unpack_body(steps, at_ref, *refs):
    count = len(steps)
    come, made = refs[:count], refs[count : 2 * count]
    w_in, w_out, held, taken, put = refs[-5:]
    for slot, step in enumerate(steps):
        @pl.when(at_ref[1] == step)
        def _():
            pltpu.make_async_copy(made[slot], held.at[slot], taken.at[slot]).start()

        @pl.when(at_ref[1] != step)
        def _():
            pltpu.make_async_copy(come[slot], held.at[slot], taken.at[slot]).start()
    for slot, step in enumerate(steps):
        pltpu.make_async_copy(come[slot], held.at[slot], taken.at[slot]).wait()
        for piece in range(4):
            @pl.when(at_ref[2 + step] == piece)
            def _():
                for target, source in piece_copies(piece, w_in, w_out, held.at[slot]):
                    pltpu.make_async_copy(source, target, put.at[slot]).start()
    for slot in range(count):
        pltpu.make_async_copy(held.at[slot], w_out.at[0], put.at[slot]).wait()


def unpack(steps, at, come, made, into=()):
    count = len(steps)
    return pl.pallas_call(
        functools.partial(unpack_body, steps),
        out_shape=(
            jax.ShapeDtypeStruct((2, 4096, 256), bf16),
            jax.ShapeDtypeStruct((2, 256, 4096), bf16),
        ),
        in_specs=[smem_spec] + [any_spec] * (2 * count + len(into)),
        out_specs=(any_spec, any_spec),
        scratch_shapes=[
            pltpu.VMEM((count, 256, 4096), bf16),
            pltpu.SemaphoreType.DMA((count,)),
            pltpu.SemaphoreType.DMA((count,)),
        ],
        input_output_aliases={1 + 2 * count + k: k for k in range(len(into))},
        compiler_params=roomy,
        cost_estimate=pl.CostEstimate(
            flops=0, bytes_accessed=count << 22, transcendentals=0
        ),
    )(at, *[come[k] for k in steps], *[made[k] for k in steps], *into)


def row_copies(at_ref, rows_in, rows, sem):
    copies = []
    for d in range(4):
        at_z = lax.rem(at_ref[6] + 4 - d, 4)
        for b in range(2):
            copies.append(
                pltpu.make_async_copy(rows_in.at[:, b, d], rows.at[:, at_z, b], sem)
            )
    return copies


def load_weights(at_ref, weights, packed, tall, wide, sems):
    def load_tall(slot, array):
        for a in range(16):
            block = pl.ds(256 * a, 256)
            target = tall.at[block, pl.ds(256 * slot, 256)]
            pltpu.make_async_copy(array.at[:, block], target, sems.at[slot]).start()

    def load_wide(slot, array):
        target = wide.at[pl.ds(256 * slot, 256), :]
        pltpu.make_async_copy(array, target, sems.at[slot]).start()

    core, own = at_ref[0], at_ref[1]
    for slot in range(4):
        for here, step, load in ((0, slot, load_tall), (1, slot ^ 1, load_wide)):
            @pl.when((core == here) & (own == step))
            def _():
                load(slot, packed[step])

            @pl.when((core == here) & (own != step))
            def _():
                load(slot, weights[step])


def wait_weights(slot, weights, wide, sems):
    pltpu.make_async_copy(weights[0], wide.at[pl.ds(256 * slot, 256), :], sems.at[slot]).wait()


def up_body(
    at_ref, rows_in, w0, w1, w2, w3, p0, p1, p2, p3,
    pre_ref, send_ref, rows, tall, wide, row_sem, sems,
):
    core = at_ref[0]
    weights = (w0, w1, w2, w3)
    for copy in row_copies(at_ref, rows_in, rows, row_sem):
        copy.start()
    load_weights(at_ref, weights, (p0, p1, p2, p3), tall, wide, sems)
    pltpu.make_async_copy(rows, rows, row_sem).wait()

    @pl.when(core == 0)
    def _():
        def slot_step(slot, carry):
            wait_weights(slot, weights, wide, sems)
            here = block_at(slot, 256)
            pre_act = mm(rows[...].reshape(512, 4096), tall[:, here])
            pre_ref[:, here] = pre_act
            send_ref[:, here] = (pre_act * jax.nn.sigmoid(pre_act)).astype(bf16)
            return carry

        lax.fori_loop(0, 4, slot_step, 0)

    @pl.when(core == 1)
    def _():
        def slot_step(slot, carry):
            wait_weights(slot, weights, wide, sems)
            here = block_at(slot, 256)
            send_ref[:, here] = mm(rows[...].reshape(512, 4096), wide[here, :], NT).astype(bf16)
            return carry

        lax.fori_loop(0, 4, slot_step, 0)


def up(at, rows, weights, packed):
    return pl.pallas_call(
        up_body,
        out_shape=(
            jax.ShapeDtypeStruct((512, 1024), f32),
            jax.ShapeDtypeStruct((512, 1024), bf16),
        ),
        in_specs=[smem_spec] + [any_spec] * 9,
        out_specs=(vmem_spec, vmem_spec),
        scratch_shapes=[
            pltpu.VMEM((8, 4, 2, 8, 4096), bf16),
            pltpu.VMEM((4096, 1024), bf16),
            pltpu.VMEM((1024, 4096), bf16),
            pltpu.SemaphoreType.DMA,
            pltpu.SemaphoreType.DMA((4,)),
        ],
        compiler_params=roomy,
        cost_estimate=pl.CostEstimate(
            flops=2 * 512 * 4096 * 1024, bytes_accessed=15 << 20, transcendentals=512 * 1024
        ),
    )(at, rows, *weights, *packed)


def down_body(
    at_ref, pre_ref, got_ref, w0, w1, w2, w3, p0, p1, p2, p3,
    part_ref, q_ref, tall, wide, sems,
):
    core = at_ref[0]
    weights = (w0, w1, w2, w3)
    load_weights(at_ref, weights, (p0, p1, p2, p3), tall, wide, sems)

    @pl.when(core == 0)
    def _():
        for slot in range(4):
            here = slice(256 * slot, 256 * slot + 256)
            pre_act = pre_ref[:, here]
            sigma_pre = jax.nn.sigmoid(pre_act)
            slope = got_ref[:, here].astype(f32) * sigma_pre * (1.0 + pre_act * (1.0 - sigma_pre))
            q_ref[:, here] = slope.astype(bf16)

    @pl.when(core == 1)
    def _():
        q_ref[...] = got_ref[...]

    for slot in range(4):
        wait_weights(slot, weights, wide, sems)

    @pl.when(core == 0)
    def _():
        for index in range(8):
            here = slice(512 * index, 512 * index + 512)
            part_ref[:, here] = mm(q_ref[...], tall[here, :], NT).astype(bf16)

    @pl.when(core == 1)
    def _():
        for index in range(8):
            here = slice(512 * index, 512 * index + 512)
            part_ref[:, here] = mm(q_ref[...], wide[:, here]).astype(bf16)


def down(at, pre_act, got, weights, packed):
    return pl.pallas_call(
        down_body,
        out_shape=(
            jax.ShapeDtypeStruct((512, 4096), bf16),
            jax.ShapeDtypeStruct((512, 1024), bf16),
        ),
        in_specs=[smem_spec] + [vmem_spec] * 2 + [any_spec] * 8,
        out_specs=(vmem_spec,) * 2,
        scratch_shapes=[
            pltpu.VMEM((4096, 1024), bf16),
            pltpu.VMEM((1024, 4096), bf16),
            pltpu.SemaphoreType.DMA((4,)),
        ],
        compiler_params=roomy,
        cost_estimate=pl.CostEstimate(
            flops=2 * 512 * 4096 * 1024, bytes_accessed=16 << 20, transcendentals=512 * 1024
        ),
    )(at, pre_act, got, *weights, *packed)


def grads_body(at_ref, rows_in, q_ref, g0, g1, g2, g3, rows, tall, wide, row_sem, sems):
    core = at_ref[0]
    grads = (g0, g1, g2, g3)
    for copy in row_copies(at_ref, rows_in, rows, row_sem):
        copy.start()
    pltpu.make_async_copy(rows, rows, row_sem).wait()

    @pl.when(core == 0)
    def _():
        def slot_step(at, carry):
            here = block_at(at, 256)
            tall[:, here] = mm(rows[...].reshape(512, 4096), q_ref[:, here], TN).astype(bf16)
            for slot in range(4):
                @pl.when(at == slot)
                def _():
                    for a in range(16):
                        block = pl.ds(256 * a, 256)
                        source = tall.at[block, pl.ds(256 * slot, 256)]
                        target = grads[slot].at[:, block]
                        pltpu.make_async_copy(source, target, sems.at[slot]).start()
            return carry

        lax.fori_loop(0, 4, slot_step, 0)

    @pl.when(core == 1)
    def _():
        def slot_step(at, carry):
            here = block_at(at, 256)
            wide[here, :] = mm(q_ref[:, here], rows[...].reshape(512, 4096), TN).astype(bf16)
            for slot in range(4):
                @pl.when(at == slot)
                def _():
                    source = wide.at[pl.ds(256 * slot, 256), :]
                    pltpu.make_async_copy(source, grads[slot ^ 1], sems.at[slot]).start()
            return carry

        lax.fori_loop(0, 4, slot_step, 0)

    for slot in range(4):
        pltpu.make_async_copy(wide.at[pl.ds(0, 256), :], grads[0], sems.at[slot]).wait()


def weight_grads(at, rows, units):
    shape = jax.ShapeDtypeStruct((256, 4096), bf16)
    return pl.pallas_call(
        grads_body,
        out_shape=(shape,) * 4,
        in_specs=[smem_spec, any_spec, vmem_spec],
        out_specs=(any_spec,) * 4,
        scratch_shapes=[
            pltpu.VMEM((8, 4, 2, 8, 4096), bf16),
            pltpu.VMEM((4096, 1024), bf16),
            pltpu.VMEM((1024, 4096), bf16),
            pltpu.SemaphoreType.DMA,
            pltpu.SemaphoreType.DMA((4,)),
        ],
        compiler_params=roomy,
        cost_estimate=pl.CostEstimate(
            flops=2 * 512 * 4096 * 1024, bytes_accessed=13 << 20, transcendentals=0
        ),
    )(at, rows, units)


def group_mask():
    column = lax.broadcasted_iota(jnp.int32, (8, 256), 1) // 2 % 8
    return (column == lax.broadcasted_iota(jnp.int32, (8, 256), 0)).astype(f32)


def dots_body(back_ref, held_ref, low_ref, high_ref, dots_ref):
    total = jnp.zeros((256, 256), f32)
    for start in range(0, 4096, 512):
        here = slice(start, start + 512)
        one, two = back_ref[:, 0, :, here], back_ref[:, 1, :, here]
        both = (one.astype(f32) + two.astype(f32)).astype(bf16).reshape(256, 512)
        target, at = (low_ref, start) if start < 2048 else (high_ref, start - 2048)
        target[:, at : at + 512] = both
        total += mm(both, held_ref[:, here], NT)
    dots_ref[...] = jnp.sum(total.reshape(32, 8, 256) * group_mask()[None], axis=1)


def sum_and_dots(back, held):
    piece = jax.ShapeDtypeStruct((256, 2048), bf16)
    return pl.pallas_call(
        dots_body,
        out_shape=(piece, piece, jax.ShapeDtypeStruct((32, 256), f32)),
        in_specs=[vmem_spec] * 2,
        out_specs=(vmem_spec,) * 3,
        compiler_params=roomy,
        cost_estimate=pl.CostEstimate(flops=1 << 29, bytes_accessed=8 << 20, transcendentals=0),
    )(back, held)


def token_body(
    at_ref, dots_ref, other_ref, spread_ref, scaled_ref, high_ref, come_ref, mixer_ref, held_ref,
    rows_ref, part_ref, value,
):
    core = at_ref[0]
    mask = group_mask()[None]
    spread, scaled = spread_ref[...], scaled_ref[...]
    d_weights = dots_ref[...] + other_ref[...]
    mixing = jnp.sum(spread, axis=1)
    column_sum = jnp.sum((mixing * d_weights)[:, None, :] * mask, axis=2, keepdims=True)
    column_sum = jnp.sum(column_sum * mask, axis=1)
    d_logits = mixing * (d_weights - column_sum) * (1.0 - scaled * scaled)
    d_high = d_logits.astype(bf16)
    d_low = (d_logits - d_high.astype(f32)).astype(bf16)
    flat = spread.reshape(256, 256)
    flat_high = flat.astype(bf16)
    flat_low = (flat - flat_high.astype(f32)).astype(bf16)
    left = jnp.concatenate([flat_high, flat_low, d_high, d_low], axis=0)

    def token_rows(half_ref, offset):
        for start in range(0, 2048, 512):
            here = slice(start, start + 512)
            half, mixer = half_ref[:, here], mixer_ref[:, offset + start : offset + start + 512]
            right = jnp.concatenate([half, half, mixer, mixer], axis=0)
            rows_ref[:, here] = mm(left, right, TN).astype(bf16)

    @pl.when(core == 0)
    def _():
        token_rows(high_ref, 2048)
        for start in range(0, 4096, 512):
            here = slice(start, start + 512)
            value[:, here] = mm(d_high, held_ref[:, here]) + mm(d_low, held_ref[:, here])
        for row in range(4):
            for at in range(32):
                part_ref[32 * row + at] = value[8 * row : 8 * row + 8, 128 * at : 128 * at + 128]

    @pl.when(core == 1)
    def _():
        token_rows(come_ref, 0)
        part_ref[...] = jnp.zeros_like(part_ref)


def token_grads(at, *arrays):
    return pl.pallas_call(
        token_body,
        out_shape=(
            jax.ShapeDtypeStruct((256, 2048), bf16),
            jax.ShapeDtypeStruct((128, 8, 128), f32),
        ),
        in_specs=[smem_spec] + [vmem_spec] * 8,
        out_specs=(vmem_spec,) * 2,
        scratch_shapes=[pltpu.VMEM((32, 4096), f32)],
        compiler_params=roomy,
        cost_estimate=pl.CostEstimate(flops=1 << 29, bytes_accessed=6 << 20, transcendentals=0),
    )(at, *arrays)


def shards(tokens, cotangent, group_of, mixer, w_in, w_out):
    seqs, positions, width = tokens.shape
    rows = seqs * positions
    core = lax.axis_index("core")
    first = core == 0
    half = width // 2
    plane = lax.axis_index("z")
    at = jnp.stack(
        [core, own_step(core, plane)] + [piece_of(step, plane) for step in range(4)] + [plane]
    ).astype(jnp.int32)
    tie = lax.optimization_barrier

    home = group_of % 16
    earlier = jnp.arange(seqs)[:, None] > jnp.arange(seqs)[None, :]
    same = (home[:, None, :] == home[None, :, :]) & earlier[:, :, None]
    member = jnp.sum(same.astype(jnp.int32), axis=1)
    place = home * 8 + jnp.arange(positions, dtype=jnp.int32)[None, :] * 2 + member
    place = place.reshape(1, rows)
    sent, *packed = sort_and_pack(
        at, place, tokens.reshape(rows, width), cotangent.reshape(rows, width), w_in, w_out
    )
    hot = (place == jnp.arange(rows, dtype=jnp.int32)[:, None]).astype(bf16)
    held = exchange(sent.reshape(16, 16, width), owners).reshape(256, width)

    def send_weights(step, piece):
        return lax.ppermute(piece, column, weight_round(step))

    weights = [send_weights(0, packed[0]), send_weights(1, packed[1])]

    planes = [(plane + d) % 4 for d in range(4)]
    mixer_e = mixer.T.reshape(8, 4, width)
    mixer_t = jnp.concatenate(
        [lax.dynamic_index_in_dim(mixer_e, p, 1, keepdims=False) for p in planes], axis=0
    )
    logits = mm(mixer_t, held, NT)
    logits = jnp.where(first, logits, lax.ppermute(logits, "core", swap))
    scaled = jnp.tanh(logits / soft_cap)
    exponent = jnp.exp(soft_cap * scaled)
    column_of = jnp.arange(256, dtype=jnp.int32) // 2 % 8
    mask = (column_of[None, :] == jnp.arange(8, dtype=jnp.int32)[:, None]).astype(f32)
    spread = exponent[:, None, :] * mask[None]
    spread = spread / jnp.sum(spread, axis=2, keepdims=True)
    spread_high, spread_low = split_high_low(spread)
    flat_high, flat_low = spread_high.reshape(256, 256), spread_low.reshape(256, 256)

    def shift(by):
        return [(s, (s + by) % 4) for s in range(4)]

    mix = (mm(flat_high, held) + mm(flat_low, held)).astype(bf16)
    blocks = {}
    for d in (2, 1, 3, 0):
        block = mix[64 * d : 64 * d + 64]
        blocks[d] = lax.ppermute(block, "z", shift(d)) if d else block
    blocks[2], weights[0], weights[1], *later = tie(
        (blocks[2], weights[0], weights[1], *packed[2:])
    )
    weights += [send_weights(step + 2, piece) for step, piece in enumerate(later)]
    sent = jnp.stack([blocks[d].reshape(8, 8, width) for d in range(4)], axis=1)
    sent = jnp.broadcast_to(sent[:, None], (8, 2, 4, 8, width)).reshape(16, 32, width)
    expert_rows = exchange(sent, near).reshape(8, 2, 4, 8, width)

    pre_act, given = up(at, expert_rows, weights, packed)
    got = lax.ppermute(given, "core", swap)
    part, units = down(at, pre_act, got, weights, packed)
    made = weight_grads(at, expert_rows, units)
    back = exchange(part.reshape(64, 8, width), same_core)

    def send_grads(step, piece):
        return lax.ppermute(piece, column, back_round(step))

    grads = [send_grads(0, made[0]), send_grads(1, made[1])]
    back, *later = tie((back, *made[2:]))

    def whole_order(array):
        split = array.reshape(4, 8, *array.shape[1:])
        order = [
            lax.dynamic_index_in_dim(split, (e - plane) % 4, 0, keepdims=False) for e in range(4)
        ]
        return jnp.stack(order, axis=1).reshape(array.shape)

    spread_e, scaled_e = whole_order(spread), whole_order(scaled)
    low, high, dots = sum_and_dots(back.reshape(32, 2, 8, width), held)
    come = lax.ppermute(low, "core", swap)
    dots_other = lax.ppermute(dots, "core", swap)
    grad_rows, mixer_part = token_grads(
        at, dots, dots_other, spread_e, scaled_e, high, come, mixer.T, held
    )
    grads.append(send_grads(2, later[0]))
    grad_rows = exchange(grad_rows.reshape(16, 16, half), owners)
    grad_rows, mixer_part, grads[0], grads[1], last = tie(
        (grad_rows, mixer_part, grads[0], grads[1], later[1])
    )
    pieces = exchange(mixer_part, axes)
    grads.append(send_grads(3, last))
    pieces, grads[2] = tie((pieces, grads[2]))
    total = jnp.sum(pieces, axis=0, keepdims=True)
    whole = exchange(jnp.broadcast_to(total, (128, 8, 128)), axes)
    grad_mixer = whole.reshape(4, 32, 8, 128).transpose(1, 3, 0, 2).reshape(width, 32)

    most = unpack((0, 1, 2), at, grads, made)
    grad_in, grad_out = unpack((3,), at, grads, made, most)
    grad_rows = grad_rows.reshape(8, 2, 16, half)
    grad_tokens = jnp.concatenate(
        [mm(hot, grad_rows[:, 1 - side].reshape(rows, half), TN).astype(bf16) for side in range(2)],
        axis=1,
    ).reshape(seqs, positions, width)
    return (grad_tokens, grad_mixer, grad_in, grad_out)


def solution(mesh):
    fine = Mesh(mesh.devices.reshape(sizes), axes)
    dp, expert = ("yh", "x", "core"), ("z", "b")
    every = dp + expert
    return jax.shard_map(
        shards,
        mesh=fine,
        in_specs=(
            P(every, None, None),
            P(every, None, None),
            P(every, None),
            P(),
            P(dp, None, expert),
            P(dp, expert, None),
        ),
        out_specs=(
            P(every, None, None),
            P(),
            P(dp, None, expert),
            P(dp, expert, None),
        ),
        check_vma=False,
    )
```

```python
import functools

import jax
import jax.numpy as jnp
from jax import lax
from jax.experimental import pallas as pl
from jax.experimental.pallas import tpu as pltpu
from jax.sharding import Mesh
from jax.sharding import PartitionSpec as P

soft_cap = 15.0
f32 = jnp.float32
bf16 = jnp.bfloat16

axes = ("yh", "x", "core", "z", "b")
sizes = (2, 4, 2, 4, 2)
owners = ("yh", "x", "core")
near = ("yh", "x", "b")
same_core = ("yh", "x", "z", "b")
column = ("core", "z")
swap = [(0, 1), (1, 0)]
NN = ((1,), (0,))
NT = ((1,), (1,))
TN = ((0,), (0,))

any_spec = pl.BlockSpec(memory_space=pl.ANY)
vmem_spec = pl.BlockSpec(memory_space=pltpu.VMEM)
smem_spec = pl.BlockSpec(memory_space=pltpu.SMEM)
roomy = pltpu.CompilerParams(vmem_limit_bytes=48 * 1024 * 1024)


def block_at(index, size):
    return pl.ds(pl.multiple_of(index * size, size), size)


def mm(left, right, contract=NN):
    return lax.dot_general(left, right, (contract, ((), ())), preferred_element_type=f32)


def exchange(array, names):
    return lax.all_to_all(array, names, split_axis=0, concat_axis=0, tiled=True)


def split_high_low(value):
    high = lax.reduce_precision(value, 8, 7)
    return high.astype(bf16), (value - high).astype(bf16)


def piece_of(step, z):
    return ((z + 1 + step // 2) % 2) * 2 + (step + z // 2) % 2


def weight_round(step):
    pairs = []
    for s in range(2):
        for z in range(4):
            q = piece_of(step, z)
            pairs.append((s * 4 + z, (q % 2) * 4 + 2 * s + q // 2))
    return [(a, b) for a, b in pairs if a != b]


def own_step(core, z):
    return jnp.where(z // 2 == core, 2, -1)


def back_round(step):
    return [(b, a) for a, b in weight_round(step)]


def piece_copies(piece, w_in, w_out, packed):
    expert = piece // 2
    if piece % 2 == 1:
        return [(w_out.at[expert], packed)]
    return [
        (w_in.at[expert, pl.ds(256 * a, 256), :], packed.at[:, pl.ds(256 * a, 256)])
        for a in range(16)
    ]


def pack_body(first, at_ref, w_in, w_out, p0, p1, held, taken, put):
    packed = (p0, p1)
    for slot in range(2):
        for piece in range(4):
            @pl.when(at_ref[2 + first + slot] == piece)
            def _():
                for source, target in piece_copies(piece, w_in, w_out, held.at[slot]):
                    pltpu.make_async_copy(source, target, taken.at[slot]).start()
    for slot in range(2):
        pltpu.make_async_copy(w_out.at[0], held.at[slot], taken.at[slot]).wait()
        pltpu.make_async_copy(held.at[slot], packed[slot], put.at[slot]).start()
    for slot in range(2):
        pltpu.make_async_copy(held.at[slot], packed[slot], put.at[slot]).wait()


def pack(first, at, w_in, w_out):
    return pl.pallas_call(
        functools.partial(pack_body, first),
        out_shape=(jax.ShapeDtypeStruct((256, 4096), bf16),) * 2,
        in_specs=[smem_spec] + [any_spec] * 2,
        out_specs=(any_spec,) * 2,
        scratch_shapes=[
            pltpu.VMEM((2, 256, 4096), bf16),
            pltpu.SemaphoreType.DMA((2,)),
            pltpu.SemaphoreType.DMA((2,)),
        ],
        compiler_params=roomy,
        cost_estimate=pl.CostEstimate(flops=0, bytes_accessed=8 << 20, transcendentals=0),
    )(at, w_in, w_out)


def sort_body(place_ref, tokens, cotangent, sent):
    rows = tokens.shape[0]
    hot = (lax.broadcasted_iota(jnp.int32, (rows, rows), 0) == place_ref[...]).astype(bf16)
    for start in range(0, tokens.shape[1], 512):
        here = pl.ds(start, 512)
        sent[:, 0, :, here] = mm(hot, tokens[:, here]).astype(bf16).reshape(8, 16, 512)
        sent[:, 1, :, here] = mm(hot, cotangent[:, here]).astype(bf16).reshape(8, 16, 512)


def sort(place, tokens, cotangent):
    return pl.pallas_call(
        sort_body,
        out_shape=jax.ShapeDtypeStruct((8, 2, 16, 4096), bf16),
        in_specs=[vmem_spec] * 3,
        out_specs=vmem_spec,
        compiler_params=roomy,
        cost_estimate=pl.CostEstimate(flops=1 << 28, bytes_accessed=4 << 20, transcendentals=0),
    )(place, tokens, cotangent)


def unpack_body(steps, at_ref, *refs):
    count = len(steps)
    come, made = refs[:count], refs[count : 2 * count]
    w_in, w_out, held, taken, put = refs[-5:]
    for slot, step in enumerate(steps):
        @pl.when(at_ref[1] == step)
        def _():
            pltpu.make_async_copy(made[slot], held.at[slot], taken.at[slot]).start()

        @pl.when(at_ref[1] != step)
        def _():
            pltpu.make_async_copy(come[slot], held.at[slot], taken.at[slot]).start()
    for slot, step in enumerate(steps):
        pltpu.make_async_copy(come[slot], held.at[slot], taken.at[slot]).wait()
        for piece in range(4):
            @pl.when(at_ref[2 + step] == piece)
            def _():
                for target, source in piece_copies(piece, w_in, w_out, held.at[slot]):
                    pltpu.make_async_copy(source, target, put.at[slot]).start()
    for slot in range(count):
        pltpu.make_async_copy(held.at[slot], w_out.at[0], put.at[slot]).wait()


def unpack(steps, at, come, made, into=()):
    count = len(steps)
    return pl.pallas_call(
        functools.partial(unpack_body, steps),
        out_shape=(
            jax.ShapeDtypeStruct((2, 4096, 256), bf16),
            jax.ShapeDtypeStruct((2, 256, 4096), bf16),
        ),
        in_specs=[smem_spec] + [any_spec] * (2 * count + len(into)),
        out_specs=(any_spec, any_spec),
        scratch_shapes=[
            pltpu.VMEM((count, 256, 4096), bf16),
            pltpu.SemaphoreType.DMA((count,)),
            pltpu.SemaphoreType.DMA((count,)),
        ],
        input_output_aliases={1 + 2 * count + k: k for k in range(len(into))},
        compiler_params=roomy,
        cost_estimate=pl.CostEstimate(
            flops=0, bytes_accessed=count << 22, transcendentals=0
        ),
    )(at, *[come[k] for k in steps], *[made[k] for k in steps], *into)


def row_copies(at_ref, rows_in, rows, sem):
    copies = []
    for d in range(4):
        at_z = lax.rem(at_ref[6] + 4 - d, 4)
        for b in range(2):
            copies.append(
                pltpu.make_async_copy(rows_in.at[:, b, d], rows.at[:, at_z, b], sem)
            )
    return copies


def load_weights(at_ref, weights, packed, tall, wide, sems):
    def load_tall(slot, array):
        for a in range(16):
            block = pl.ds(256 * a, 256)
            target = tall.at[block, pl.ds(256 * slot, 256)]
            pltpu.make_async_copy(array.at[:, block], target, sems.at[slot]).start()

    def load_wide(slot, array):
        target = wide.at[pl.ds(256 * slot, 256), :]
        pltpu.make_async_copy(array, target, sems.at[slot]).start()

    core, own = at_ref[0], at_ref[1]
    for slot in range(4):
        for here, step, load in ((0, slot, load_tall), (1, slot ^ 1, load_wide)):
            @pl.when((core == here) & (own == step))
            def _():
                load(slot, packed[step])

            @pl.when((core == here) & (own != step))
            def _():
                load(slot, weights[step])


def wait_weights(slot, weights, wide, sems):
    pltpu.make_async_copy(weights[0], wide.at[pl.ds(256 * slot, 256), :], sems.at[slot]).wait()


def up_body(
    at_ref, rows_in, w0, w1, w2, w3, p0, p1, p2, p3,
    pre_ref, send_ref, rows, tall, wide, row_sem, sems,
):
    core = at_ref[0]
    weights = (w0, w1, w2, w3)
    for copy in row_copies(at_ref, rows_in, rows, row_sem):
        copy.start()
    load_weights(at_ref, weights, (p0, p1, p2, p3), tall, wide, sems)
    pltpu.make_async_copy(rows, rows, row_sem).wait()

    @pl.when(core == 0)
    def _():
        def slot_step(slot, carry):
            wait_weights(slot, weights, wide, sems)
            here = block_at(slot, 256)
            pre_act = mm(rows[...].reshape(512, 4096), tall[:, here])
            pre_ref[:, here] = pre_act
            send_ref[:, here] = (pre_act * jax.nn.sigmoid(pre_act)).astype(bf16)
            return carry

        lax.fori_loop(0, 4, slot_step, 0)

    @pl.when(core == 1)
    def _():
        def slot_step(slot, carry):
            wait_weights(slot, weights, wide, sems)
            here = block_at(slot, 256)
            send_ref[:, here] = mm(rows[...].reshape(512, 4096), wide[here, :], NT).astype(bf16)
            return carry

        lax.fori_loop(0, 4, slot_step, 0)


def up(at, rows, weights, packed):
    return pl.pallas_call(
        up_body,
        out_shape=(
            jax.ShapeDtypeStruct((512, 1024), f32),
            jax.ShapeDtypeStruct((512, 1024), bf16),
        ),
        in_specs=[smem_spec] + [any_spec] * 9,
        out_specs=(vmem_spec, vmem_spec),
        scratch_shapes=[
            pltpu.VMEM((8, 4, 2, 8, 4096), bf16),
            pltpu.VMEM((4096, 1024), bf16),
            pltpu.VMEM((1024, 4096), bf16),
            pltpu.SemaphoreType.DMA,
            pltpu.SemaphoreType.DMA((4,)),
        ],
        compiler_params=roomy,
        cost_estimate=pl.CostEstimate(
            flops=2 * 512 * 4096 * 1024, bytes_accessed=15 << 20, transcendentals=512 * 1024
        ),
    )(at, rows, *weights, *packed)


def down_body(
    at_ref, pre_ref, got_ref, w0, w1, w2, w3, p0, p1, p2, p3,
    part, q_ref, tall, wide, part_ref, part_sem, sems,
):
    core = at_ref[0]
    weights = (w0, w1, w2, w3)
    load_weights(at_ref, weights, (p0, p1, p2, p3), tall, wide, sems)

    @pl.when(core == 0)
    def _():
        for slot in range(4):
            here = slice(256 * slot, 256 * slot + 256)
            pre_act = pre_ref[:, here]
            sigma_pre = jax.nn.sigmoid(pre_act)
            slope = got_ref[:, here].astype(f32) * sigma_pre * (1.0 + pre_act * (1.0 - sigma_pre))
            q_ref[:, here] = slope.astype(bf16)

    @pl.when(core == 1)
    def _():
        q_ref[...] = got_ref[...]

    for slot in range(4):
        wait_weights(slot, weights, wide, sems)

    def put(here):
        here = pl.ds(here.start, 512)
        pltpu.make_async_copy(part_ref.at[:, here], part.at[:, here], part_sem).start()

    @pl.when(core == 0)
    def _():
        for index in range(8):
            here = slice(512 * index, 512 * index + 512)
            part_ref[:, here] = mm(q_ref[...], tall[here, :], NT).astype(bf16)
            put(here)

    @pl.when(core == 1)
    def _():
        for index in range(8):
            here = slice(512 * index, 512 * index + 512)
            part_ref[:, here] = mm(q_ref[...], wide[:, here]).astype(bf16)
            put(here)

    pltpu.make_async_copy(part_ref, part, part_sem).wait()


def down(at, pre_act, got, weights, packed):
    return pl.pallas_call(
        down_body,
        out_shape=(
            jax.ShapeDtypeStruct((512, 4096), bf16),
            jax.ShapeDtypeStruct((512, 1024), bf16),
        ),
        in_specs=[smem_spec] + [vmem_spec] * 2 + [any_spec] * 8,
        out_specs=(any_spec, vmem_spec),
        scratch_shapes=[
            pltpu.VMEM((4096, 1024), bf16),
            pltpu.VMEM((1024, 4096), bf16),
            pltpu.VMEM((512, 4096), bf16),
            pltpu.SemaphoreType.DMA,
            pltpu.SemaphoreType.DMA((4,)),
        ],
        compiler_params=roomy,
        cost_estimate=pl.CostEstimate(
            flops=2 * 512 * 4096 * 1024, bytes_accessed=16 << 20, transcendentals=512 * 1024
        ),
    )(at, pre_act, got, *weights, *packed)


def grads_body(at_ref, rows_in, q_ref, g0, g1, g2, g3, rows, tall, wide, row_sem, sems):
    core = at_ref[0]
    grads = (g0, g1, g2, g3)
    for copy in row_copies(at_ref, rows_in, rows, row_sem):
        copy.start()
    pltpu.make_async_copy(rows, rows, row_sem).wait()

    @pl.when(core == 0)
    def _():
        def slot_step(at, carry):
            here = block_at(at, 256)
            tall[:, here] = mm(rows[...].reshape(512, 4096), q_ref[:, here], TN).astype(bf16)
            for slot in range(4):
                @pl.when(at == slot)
                def _():
                    for a in range(16):
                        block = pl.ds(256 * a, 256)
                        source = tall.at[block, pl.ds(256 * slot, 256)]
                        target = grads[slot].at[:, block]
                        pltpu.make_async_copy(source, target, sems.at[slot]).start()
            return carry

        lax.fori_loop(0, 4, slot_step, 0)

    @pl.when(core == 1)
    def _():
        def slot_step(at, carry):
            here = block_at(at, 256)
            wide[here, :] = mm(q_ref[:, here], rows[...].reshape(512, 4096), TN).astype(bf16)
            for slot in range(4):
                @pl.when(at == slot)
                def _():
                    source = wide.at[pl.ds(256 * slot, 256), :]
                    pltpu.make_async_copy(source, grads[slot ^ 1], sems.at[slot]).start()
            return carry

        lax.fori_loop(0, 4, slot_step, 0)

    for slot in range(4):
        pltpu.make_async_copy(wide.at[pl.ds(0, 256), :], grads[0], sems.at[slot]).wait()


def weight_grads(at, rows, units):
    shape = jax.ShapeDtypeStruct((256, 4096), bf16)
    return pl.pallas_call(
        grads_body,
        out_shape=(shape,) * 4,
        in_specs=[smem_spec, any_spec, vmem_spec],
        out_specs=(any_spec,) * 4,
        scratch_shapes=[
            pltpu.VMEM((8, 4, 2, 8, 4096), bf16),
            pltpu.VMEM((4096, 1024), bf16),
            pltpu.VMEM((1024, 4096), bf16),
            pltpu.SemaphoreType.DMA,
            pltpu.SemaphoreType.DMA((4,)),
        ],
        compiler_params=roomy,
        cost_estimate=pl.CostEstimate(
            flops=2 * 512 * 4096 * 1024, bytes_accessed=13 << 20, transcendentals=0
        ),
    )(at, rows, units)


def group_mask():
    column = lax.broadcasted_iota(jnp.int32, (8, 256), 1) // 2 % 8
    return (column == lax.broadcasted_iota(jnp.int32, (8, 256), 0)).astype(f32)


def dots_body(back_ref, held_ref, low_ref, high_ref, dots_ref):
    total = jnp.zeros((256, 256), f32)
    for start in range(0, 4096, 512):
        here = slice(start, start + 512)
        one, two = back_ref[:, 0, :, here], back_ref[:, 1, :, here]
        both = (one.astype(f32) + two.astype(f32)).astype(bf16).reshape(256, 512)
        target, at = (low_ref, start) if start < 2048 else (high_ref, start - 2048)
        target[:, at : at + 512] = both
        total += mm(both, held_ref[:, here], NT)
    dots_ref[...] = jnp.sum(total.reshape(32, 8, 256) * group_mask()[None], axis=1)


def sum_and_dots(back, held):
    piece = jax.ShapeDtypeStruct((256, 2048), bf16)
    return pl.pallas_call(
        dots_body,
        out_shape=(piece, piece, jax.ShapeDtypeStruct((32, 256), f32)),
        in_specs=[vmem_spec] * 2,
        out_specs=(vmem_spec,) * 3,
        compiler_params=roomy,
        cost_estimate=pl.CostEstimate(flops=1 << 29, bytes_accessed=8 << 20, transcendentals=0),
    )(back, held)


def token_body(
    at_ref, dots_ref, other_ref, spread_ref, scaled_ref, high_ref, come_ref, mixer_ref, held_ref,
    rows_ref, part_ref, value,
):
    core = at_ref[0]
    mask = group_mask()[None]
    spread, scaled = spread_ref[...], scaled_ref[...]
    d_weights = dots_ref[...] + other_ref[...]
    mixing = jnp.sum(spread, axis=1)
    column_sum = jnp.sum((mixing * d_weights)[:, None, :] * mask, axis=2, keepdims=True)
    column_sum = jnp.sum(column_sum * mask, axis=1)
    d_logits = mixing * (d_weights - column_sum) * (1.0 - scaled * scaled)
    d_high = d_logits.astype(bf16)
    d_low = (d_logits - d_high.astype(f32)).astype(bf16)
    flat = spread.reshape(256, 256)
    flat_high = flat.astype(bf16)
    flat_low = (flat - flat_high.astype(f32)).astype(bf16)
    left = jnp.concatenate([flat_high, flat_low, d_high, d_low], axis=0)

    def token_rows(half_ref, offset):
        for start in range(0, 2048, 512):
            here = slice(start, start + 512)
            half, mixer = half_ref[:, here], mixer_ref[:, offset + start : offset + start + 512]
            right = jnp.concatenate([half, half, mixer, mixer], axis=0)
            rows_ref[:, here] = mm(left, right, TN).astype(bf16)

    @pl.when(core == 0)
    def _():
        token_rows(high_ref, 2048)
        for start in range(0, 4096, 512):
            here = slice(start, start + 512)
            value[:, here] = mm(d_high, held_ref[:, here]) + mm(d_low, held_ref[:, here])
        for row in range(4):
            for at in range(32):
                part_ref[32 * row + at] = value[8 * row : 8 * row + 8, 128 * at : 128 * at + 128]

    @pl.when(core == 1)
    def _():
        token_rows(come_ref, 0)
        part_ref[...] = jnp.zeros_like(part_ref)


def token_grads(at, *arrays):
    return pl.pallas_call(
        token_body,
        out_shape=(
            jax.ShapeDtypeStruct((256, 2048), bf16),
            jax.ShapeDtypeStruct((128, 8, 128), f32),
        ),
        in_specs=[smem_spec] + [vmem_spec] * 8,
        out_specs=(vmem_spec,) * 2,
        scratch_shapes=[pltpu.VMEM((32, 4096), f32)],
        compiler_params=roomy,
        cost_estimate=pl.CostEstimate(flops=1 << 29, bytes_accessed=6 << 20, transcendentals=0),
    )(at, *arrays)


def shards(tokens, cotangent, group_of, mixer, w_in, w_out):
    seqs, positions, width = tokens.shape
    rows = seqs * positions
    core = lax.axis_index("core")
    first = core == 0
    half = width // 2
    plane = lax.axis_index("z")
    at = jnp.stack(
        [core, own_step(core, plane)] + [piece_of(step, plane) for step in range(4)] + [plane]
    ).astype(jnp.int32)
    tie = lax.optimization_barrier

    home = group_of % 16
    earlier = jnp.arange(seqs)[:, None] > jnp.arange(seqs)[None, :]
    same = (home[:, None, :] == home[None, :, :]) & earlier[:, :, None]
    member = jnp.sum(same.astype(jnp.int32), axis=1)
    place = home * 8 + jnp.arange(positions, dtype=jnp.int32)[None, :] * 2 + member
    place = place.reshape(1, rows)
    packed = pack(0, at, w_in, w_out)
    place, *packed = tie((place, *packed))
    sent = sort(place, tokens.reshape(rows, width), cotangent.reshape(rows, width))
    hot = (place == jnp.arange(rows, dtype=jnp.int32)[:, None]).astype(bf16)
    held = exchange(sent.reshape(16, 16, width), owners).reshape(256, width)

    def send_weights(step, piece):
        return lax.ppermute(piece, column, weight_round(step))

    weights = [send_weights(0, packed[0])]
    weights[0], second = tie((weights[0], packed[1]))
    weights.append(send_weights(1, second))
    packed += pack(2, at, w_in, w_out)

    planes = [(plane + d) % 4 for d in range(4)]
    mixer_e = mixer.T.reshape(8, 4, width)
    mixer_t = jnp.concatenate(
        [lax.dynamic_index_in_dim(mixer_e, p, 1, keepdims=False) for p in planes], axis=0
    )
    logits = mm(mixer_t, held, NT)
    logits = jnp.where(first, logits, lax.ppermute(logits, "core", swap))
    scaled = jnp.tanh(logits / soft_cap)
    exponent = jnp.exp(soft_cap * scaled)
    column_of = jnp.arange(256, dtype=jnp.int32) // 2 % 8
    mask = (column_of[None, :] == jnp.arange(8, dtype=jnp.int32)[:, None]).astype(f32)
    spread = exponent[:, None, :] * mask[None]
    spread = spread / jnp.sum(spread, axis=2, keepdims=True)
    spread_high, spread_low = split_high_low(spread)
    flat_high, flat_low = spread_high.reshape(256, 256), spread_low.reshape(256, 256)

    def shift(by):
        return [(s, (s + by) % 4) for s in range(4)]

    mix = (mm(flat_high, held) + mm(flat_low, held)).astype(bf16)
    mix, weights[1] = tie((mix, weights[1]))
    blocks = {}
    for d in (2, 1, 3, 0):
        block = mix[64 * d : 64 * d + 64]
        blocks[d] = lax.ppermute(block, "z", shift(d)) if d else block
    blocks[2], *later = tie((blocks[2], *packed[2:]))
    weights += [send_weights(step + 2, piece) for step, piece in enumerate(later)]
    sent = jnp.stack([blocks[d].reshape(8, 8, width) for d in range(4)], axis=1)
    sent = jnp.broadcast_to(sent[:, None], (8, 2, 4, 8, width)).reshape(16, 32, width)
    expert_rows = exchange(sent, near).reshape(8, 2, 4, 8, width)

    pre_act, given = up(at, expert_rows, weights, packed)
    got = lax.ppermute(given, "core", swap)
    part, units = down(at, pre_act, got, weights, packed)
    made = weight_grads(at, expert_rows, units)
    back = exchange(part.reshape(64, 8, width), same_core)

    def send_grads(step, piece):
        return lax.ppermute(piece, column, back_round(step))

    grads = [send_grads(0, made[0]), send_grads(1, made[1])]
    back, *later = tie((back, *made[2:]))

    def whole_order(array):
        split = array.reshape(4, 8, *array.shape[1:])
        order = [
            lax.dynamic_index_in_dim(split, (e - plane) % 4, 0, keepdims=False) for e in range(4)
        ]
        return jnp.stack(order, axis=1).reshape(array.shape)

    spread_e, scaled_e = whole_order(spread), whole_order(scaled)
    low, high, dots = sum_and_dots(back.reshape(32, 2, 8, width), held)
    come = lax.ppermute(low, "core", swap)
    dots_other = lax.ppermute(dots, "core", swap)
    grad_rows, mixer_part = token_grads(
        at, dots, dots_other, spread_e, scaled_e, high, come, mixer.T, held
    )
    grads.append(send_grads(2, later[0]))
    grad_rows = exchange(grad_rows.reshape(16, 16, half), owners)
    grad_rows, mixer_part, grads[0] = tie((grad_rows, mixer_part, grads[0]))
    pieces = exchange(mixer_part, axes)
    pieces, grads[1], grads[2], last = tie((pieces, grads[1], grads[2], later[1]))
    grads.append(send_grads(3, last))
    total = jnp.sum(pieces, axis=0, keepdims=True)
    whole = exchange(jnp.broadcast_to(total, (128, 8, 128)), axes)
    grad_mixer = whole.reshape(4, 32, 8, 128).transpose(1, 3, 0, 2).reshape(width, 32)

    most = unpack((0, 1, 2), at, grads, made)
    grad_in, grad_out = unpack((3,), at, grads, made, most)
    grad_rows = grad_rows.reshape(8, 2, 16, half)
    grad_tokens = jnp.concatenate(
        [mm(hot, grad_rows[:, 1 - side].reshape(rows, half), TN).astype(bf16) for side in range(2)],
        axis=1,
    ).reshape(seqs, positions, width)
    return (grad_tokens, grad_mixer, grad_in, grad_out)


def solution(mesh):
    fine = Mesh(mesh.devices.reshape(sizes), axes)
    dp, expert = ("yh", "x", "core"), ("z", "b")
    every = dp + expert
    return jax.shard_map(
        shards,
        mesh=fine,
        in_specs=(
            P(every, None, None),
            P(every, None, None),
            P(every, None),
            P(),
            P(dp, None, expert),
            P(dp, expert, None),
        ),
        out_specs=(
            P(every, None, None),
            P(),
            P(dp, None, expert),
            P(dp, expert, None),
        ),
        check_vma=False,
    )
```

```python
import functools

import jax
import jax.numpy as jnp
from jax import lax
from jax.experimental import pallas as pl
from jax.experimental.pallas import tpu as pltpu
from jax.sharding import Mesh
from jax.sharding import PartitionSpec as P

soft_cap = 15.0
f32 = jnp.float32
bf16 = jnp.bfloat16

axes = ("yh", "x", "core", "z", "b")
sizes = (2, 4, 2, 4, 2)
owners = ("yh", "x", "core")
near = ("yh", "x", "b")
same_core = ("yh", "x", "z", "b")
column = ("core", "z")
swap = [(0, 1), (1, 0)]
NN = ((1,), (0,))
NT = ((1,), (1,))
TN = ((0,), (0,))

any_spec = pl.BlockSpec(memory_space=pl.ANY)
vmem_spec = pl.BlockSpec(memory_space=pltpu.VMEM)
smem_spec = pl.BlockSpec(memory_space=pltpu.SMEM)
roomy = pltpu.CompilerParams(vmem_limit_bytes=48 * 1024 * 1024)


def block_at(index, size):
    return pl.ds(pl.multiple_of(index * size, size), size)


def mm(left, right, contract=NN):
    return lax.dot_general(left, right, (contract, ((), ())), preferred_element_type=f32)


def exchange(array, names):
    return lax.all_to_all(array, names, split_axis=0, concat_axis=0, tiled=True)


def split_high_low(value):
    high = lax.reduce_precision(value, 8, 7)
    return high.astype(bf16), (value - high).astype(bf16)


def piece_of(step, z):
    return ((z + 1 + step // 2) % 2) * 2 + (step + z // 2) % 2


def weight_round(step):
    pairs = []
    for s in range(2):
        for z in range(4):
            q = piece_of(step, z)
            pairs.append((s * 4 + z, (q % 2) * 4 + 2 * s + q // 2))
    return [(a, b) for a, b in pairs if a != b]


def own_step(core, z):
    return jnp.where(z // 2 == core, 2, -1)


def back_round(step):
    return [(b, a) for a, b in weight_round(step)]


def piece_copies(piece, w_in, w_out, packed):
    expert = piece // 2
    if piece % 2 == 1:
        return [(w_out.at[expert], packed)]
    return [
        (w_in.at[expert, pl.ds(256 * a, 256), :], packed.at[:, pl.ds(256 * a, 256)])
        for a in range(16)
    ]


def pack_body(steps, at_ref, w_in, w_out, *refs):
    count = len(steps)
    packed, (held, taken, put) = refs[:count], refs[count:]
    for slot, step in enumerate(steps):
        for piece in range(4):
            @pl.when(at_ref[2 + step] == piece)
            def _():
                for source, target in piece_copies(piece, w_in, w_out, held.at[slot]):
                    pltpu.make_async_copy(source, target, taken.at[slot]).start()
    for slot in range(count):
        pltpu.make_async_copy(w_out.at[0], held.at[slot], taken.at[slot]).wait()
        pltpu.make_async_copy(held.at[slot], packed[slot], put.at[slot]).start()
    for slot in range(count):
        pltpu.make_async_copy(held.at[slot], packed[slot], put.at[slot]).wait()


def pack(steps, at, w_in, w_out):
    count = len(steps)
    return list(
        pl.pallas_call(
            functools.partial(pack_body, steps),
            out_shape=(jax.ShapeDtypeStruct((256, 4096), bf16),) * count,
            in_specs=[smem_spec] + [any_spec] * 2,
            out_specs=(any_spec,) * count,
            scratch_shapes=[
                pltpu.VMEM((count, 256, 4096), bf16),
                pltpu.SemaphoreType.DMA((count,)),
                pltpu.SemaphoreType.DMA((count,)),
            ],
            compiler_params=roomy,
            cost_estimate=pl.CostEstimate(
                flops=0, bytes_accessed=count << 22, transcendentals=0
            ),
        )(at, w_in, w_out)
    )


def sort_body(place_ref, tokens, cotangent, sent):
    rows = tokens.shape[0]
    hot = (lax.broadcasted_iota(jnp.int32, (rows, rows), 0) == place_ref[...]).astype(bf16)
    for start in range(0, tokens.shape[1], 512):
        here = pl.ds(start, 512)
        sent[:, 0, :, here] = mm(hot, tokens[:, here]).astype(bf16).reshape(8, 16, 512)
        sent[:, 1, :, here] = mm(hot, cotangent[:, here]).astype(bf16).reshape(8, 16, 512)


def sort(place, tokens, cotangent):
    return pl.pallas_call(
        sort_body,
        out_shape=jax.ShapeDtypeStruct((8, 2, 16, 4096), bf16),
        in_specs=[vmem_spec] * 3,
        out_specs=vmem_spec,
        compiler_params=roomy,
        cost_estimate=pl.CostEstimate(flops=1 << 28, bytes_accessed=4 << 20, transcendentals=0),
    )(place, tokens, cotangent)


def unpack_body(steps, at_ref, *refs):
    count = len(steps)
    come, made = refs[:count], refs[count : 2 * count]
    w_in, w_out, held, taken, put = refs[-5:]
    for slot, step in enumerate(steps):
        @pl.when(at_ref[1] == step)
        def _():
            pltpu.make_async_copy(made[slot], held.at[slot], taken.at[slot]).start()

        @pl.when(at_ref[1] != step)
        def _():
            pltpu.make_async_copy(come[slot], held.at[slot], taken.at[slot]).start()
    for slot, step in enumerate(steps):
        pltpu.make_async_copy(come[slot], held.at[slot], taken.at[slot]).wait()
        for piece in range(4):
            @pl.when(at_ref[2 + step] == piece)
            def _():
                for target, source in piece_copies(piece, w_in, w_out, held.at[slot]):
                    pltpu.make_async_copy(source, target, put.at[slot]).start()
    for slot in range(count):
        pltpu.make_async_copy(held.at[slot], w_out.at[0], put.at[slot]).wait()


def unpack(steps, at, come, made, into=()):
    count = len(steps)
    return pl.pallas_call(
        functools.partial(unpack_body, steps),
        out_shape=(
            jax.ShapeDtypeStruct((2, 4096, 256), bf16),
            jax.ShapeDtypeStruct((2, 256, 4096), bf16),
        ),
        in_specs=[smem_spec] + [any_spec] * (2 * count + len(into)),
        out_specs=(any_spec, any_spec),
        scratch_shapes=[
            pltpu.VMEM((count, 256, 4096), bf16),
            pltpu.SemaphoreType.DMA((count,)),
            pltpu.SemaphoreType.DMA((count,)),
        ],
        input_output_aliases={1 + 2 * count + k: k for k in range(len(into))},
        compiler_params=roomy,
        cost_estimate=pl.CostEstimate(
            flops=0, bytes_accessed=count << 22, transcendentals=0
        ),
    )(at, *[come[k] for k in steps], *[made[k] for k in steps], *into)


def row_copies(at_ref, rows_in, rows, sem):
    copies = []
    for d in range(4):
        at_z = lax.rem(at_ref[6] + 4 - d, 4)
        for b in range(2):
            copies.append(
                pltpu.make_async_copy(rows_in.at[:, b, d], rows.at[:, at_z, b], sem)
            )
    return copies


def load_weights(at_ref, weights, packed, tall, wide, sems):
    def load_tall(slot, array):
        for a in range(16):
            block = pl.ds(256 * a, 256)
            target = tall.at[block, pl.ds(256 * slot, 256)]
            pltpu.make_async_copy(array.at[:, block], target, sems.at[slot]).start()

    def load_wide(slot, array):
        target = wide.at[pl.ds(256 * slot, 256), :]
        pltpu.make_async_copy(array, target, sems.at[slot]).start()

    core, own = at_ref[0], at_ref[1]
    for slot in range(4):
        for here, step, load in ((0, slot, load_tall), (1, slot ^ 1, load_wide)):
            @pl.when((core == here) & (own == step))
            def _():
                load(slot, packed[step])

            @pl.when((core == here) & (own != step))
            def _():
                load(slot, weights[step])


def wait_weights(slot, weights, wide, sems):
    pltpu.make_async_copy(weights[0], wide.at[pl.ds(256 * slot, 256), :], sems.at[slot]).wait()


def up_body(
    at_ref, rows_in, w0, w1, w2, w3, p0, p1, p2, p3,
    pre_ref, send_ref, rows, tall, wide, row_sem, sems,
):
    core = at_ref[0]
    weights = (w0, w1, w2, w3)
    for copy in row_copies(at_ref, rows_in, rows, row_sem):
        copy.start()
    load_weights(at_ref, weights, (p0, p1, p2, p3), tall, wide, sems)
    pltpu.make_async_copy(rows, rows, row_sem).wait()

    @pl.when(core == 0)
    def _():
        def slot_step(slot, carry):
            wait_weights(slot, weights, wide, sems)
            here = block_at(slot, 256)
            pre_act = mm(rows[...].reshape(512, 4096), tall[:, here])
            pre_ref[:, here] = pre_act
            send_ref[:, here] = (pre_act * jax.nn.sigmoid(pre_act)).astype(bf16)
            return carry

        lax.fori_loop(0, 4, slot_step, 0)

    @pl.when(core == 1)
    def _():
        def slot_step(slot, carry):
            wait_weights(slot, weights, wide, sems)
            here = block_at(slot, 256)
            send_ref[:, here] = mm(rows[...].reshape(512, 4096), wide[here, :], NT).astype(bf16)
            return carry

        lax.fori_loop(0, 4, slot_step, 0)


def up(at, rows, weights, packed):
    return pl.pallas_call(
        up_body,
        out_shape=(
            jax.ShapeDtypeStruct((512, 1024), f32),
            jax.ShapeDtypeStruct((512, 1024), bf16),
        ),
        in_specs=[smem_spec] + [any_spec] * 9,
        out_specs=(vmem_spec, vmem_spec),
        scratch_shapes=[
            pltpu.VMEM((8, 4, 2, 8, 4096), bf16),
            pltpu.VMEM((4096, 1024), bf16),
            pltpu.VMEM((1024, 4096), bf16),
            pltpu.SemaphoreType.DMA,
            pltpu.SemaphoreType.DMA((4,)),
        ],
        compiler_params=roomy,
        cost_estimate=pl.CostEstimate(
            flops=2 * 512 * 4096 * 1024, bytes_accessed=15 << 20, transcendentals=512 * 1024
        ),
    )(at, rows, *weights, *packed)


def down_body(
    at_ref, pre_ref, got_ref, w0, w1, w2, w3, p0, p1, p2, p3,
    part, q_ref, tall, wide, part_ref, part_sem, sems,
):
    core = at_ref[0]
    weights = (w0, w1, w2, w3)
    load_weights(at_ref, weights, (p0, p1, p2, p3), tall, wide, sems)

    @pl.when(core == 0)
    def _():
        for slot in range(4):
            here = slice(256 * slot, 256 * slot + 256)
            pre_act = pre_ref[:, here]
            sigma_pre = jax.nn.sigmoid(pre_act)
            slope = got_ref[:, here].astype(f32) * sigma_pre * (1.0 + pre_act * (1.0 - sigma_pre))
            q_ref[:, here] = slope.astype(bf16)

    @pl.when(core == 1)
    def _():
        q_ref[...] = got_ref[...]

    for slot in range(4):
        wait_weights(slot, weights, wide, sems)

    def put(here):
        here = pl.ds(here.start, 512)
        pltpu.make_async_copy(part_ref.at[:, here], part.at[:, here], part_sem).start()

    @pl.when(core == 0)
    def _():
        for index in range(8):
            here = slice(512 * index, 512 * index + 512)
            part_ref[:, here] = mm(q_ref[...], tall[here, :], NT).astype(bf16)
            put(here)

    @pl.when(core == 1)
    def _():
        for index in range(8):
            here = slice(512 * index, 512 * index + 512)
            part_ref[:, here] = mm(q_ref[...], wide[:, here]).astype(bf16)
            put(here)

    pltpu.make_async_copy(part_ref, part, part_sem).wait()


def down(at, pre_act, got, weights, packed):
    return pl.pallas_call(
        down_body,
        out_shape=(
            jax.ShapeDtypeStruct((512, 4096), bf16),
            jax.ShapeDtypeStruct((512, 1024), bf16),
        ),
        in_specs=[smem_spec] + [vmem_spec] * 2 + [any_spec] * 8,
        out_specs=(any_spec, vmem_spec),
        scratch_shapes=[
            pltpu.VMEM((4096, 1024), bf16),
            pltpu.VMEM((1024, 4096), bf16),
            pltpu.VMEM((512, 4096), bf16),
            pltpu.SemaphoreType.DMA,
            pltpu.SemaphoreType.DMA((4,)),
        ],
        compiler_params=roomy,
        cost_estimate=pl.CostEstimate(
            flops=2 * 512 * 4096 * 1024, bytes_accessed=16 << 20, transcendentals=512 * 1024
        ),
    )(at, pre_act, got, *weights, *packed)


def grads_body(at_ref, rows_in, q_ref, g0, g1, g2, g3, rows, tall, wide, row_sem, sems):
    core = at_ref[0]
    grads = (g0, g1, g2, g3)
    for copy in row_copies(at_ref, rows_in, rows, row_sem):
        copy.start()
    pltpu.make_async_copy(rows, rows, row_sem).wait()

    @pl.when(core == 0)
    def _():
        def slot_step(at, carry):
            here = block_at(at, 256)
            tall[:, here] = mm(rows[...].reshape(512, 4096), q_ref[:, here], TN).astype(bf16)
            for slot in range(4):
                @pl.when(at == slot)
                def _():
                    for a in range(16):
                        block = pl.ds(256 * a, 256)
                        source = tall.at[block, pl.ds(256 * slot, 256)]
                        target = grads[slot].at[:, block]
                        pltpu.make_async_copy(source, target, sems.at[slot]).start()
            return carry

        lax.fori_loop(0, 4, slot_step, 0)

    @pl.when(core == 1)
    def _():
        def slot_step(at, carry):
            here = block_at(at, 256)
            wide[here, :] = mm(q_ref[:, here], rows[...].reshape(512, 4096), TN).astype(bf16)
            for slot in range(4):
                @pl.when(at == slot)
                def _():
                    source = wide.at[pl.ds(256 * slot, 256), :]
                    pltpu.make_async_copy(source, grads[slot ^ 1], sems.at[slot]).start()
            return carry

        lax.fori_loop(0, 4, slot_step, 0)

    for slot in range(4):
        pltpu.make_async_copy(wide.at[pl.ds(0, 256), :], grads[0], sems.at[slot]).wait()


def weight_grads(at, rows, units):
    shape = jax.ShapeDtypeStruct((256, 4096), bf16)
    return pl.pallas_call(
        grads_body,
        out_shape=(shape,) * 4,
        in_specs=[smem_spec, any_spec, vmem_spec],
        out_specs=(any_spec,) * 4,
        scratch_shapes=[
            pltpu.VMEM((8, 4, 2, 8, 4096), bf16),
            pltpu.VMEM((4096, 1024), bf16),
            pltpu.VMEM((1024, 4096), bf16),
            pltpu.SemaphoreType.DMA,
            pltpu.SemaphoreType.DMA((4,)),
        ],
        compiler_params=roomy,
        cost_estimate=pl.CostEstimate(
            flops=2 * 512 * 4096 * 1024, bytes_accessed=13 << 20, transcendentals=0
        ),
    )(at, rows, units)


def group_mask():
    column = lax.broadcasted_iota(jnp.int32, (8, 256), 1) // 2 % 8
    return (column == lax.broadcasted_iota(jnp.int32, (8, 256), 0)).astype(f32)


def dots_body(back_ref, held_ref, low_ref, high_ref, dots_ref):
    total = jnp.zeros((256, 256), f32)
    for start in range(0, 4096, 512):
        here = slice(start, start + 512)
        one, two = back_ref[:, 0, :, here], back_ref[:, 1, :, here]
        both = (one.astype(f32) + two.astype(f32)).astype(bf16).reshape(256, 512)
        target, at = (low_ref, start) if start < 2048 else (high_ref, start - 2048)
        target[:, at : at + 512] = both
        total += mm(both, held_ref[:, here], NT)
    dots_ref[...] = jnp.sum(total.reshape(32, 8, 256) * group_mask()[None], axis=1)


def sum_and_dots(back, held):
    piece = jax.ShapeDtypeStruct((256, 2048), bf16)
    return pl.pallas_call(
        dots_body,
        out_shape=(piece, piece, jax.ShapeDtypeStruct((32, 256), f32)),
        in_specs=[vmem_spec] * 2,
        out_specs=(vmem_spec,) * 3,
        compiler_params=roomy,
        cost_estimate=pl.CostEstimate(flops=1 << 29, bytes_accessed=8 << 20, transcendentals=0),
    )(back, held)


def token_body(
    at_ref, dots_ref, other_ref, spread_ref, scaled_ref, high_ref, come_ref, mixer_ref, held_ref,
    rows_ref, part_ref, value,
):
    core = at_ref[0]
    mask = group_mask()[None]
    spread, scaled = spread_ref[...], scaled_ref[...]
    d_weights = dots_ref[...] + other_ref[...]
    mixing = jnp.sum(spread, axis=1)
    column_sum = jnp.sum((mixing * d_weights)[:, None, :] * mask, axis=2, keepdims=True)
    column_sum = jnp.sum(column_sum * mask, axis=1)
    d_logits = mixing * (d_weights - column_sum) * (1.0 - scaled * scaled)
    d_high = d_logits.astype(bf16)
    d_low = (d_logits - d_high.astype(f32)).astype(bf16)
    flat = spread.reshape(256, 256)
    flat_high = flat.astype(bf16)
    flat_low = (flat - flat_high.astype(f32)).astype(bf16)
    left = jnp.concatenate([flat_high, flat_low, d_high, d_low], axis=0)

    def token_rows(half_ref, offset):
        for start in range(0, 2048, 512):
            here = slice(start, start + 512)
            half, mixer = half_ref[:, here], mixer_ref[:, offset + start : offset + start + 512]
            right = jnp.concatenate([half, half, mixer, mixer], axis=0)
            rows_ref[:, here] = mm(left, right, TN).astype(bf16)

    @pl.when(core == 0)
    def _():
        token_rows(high_ref, 2048)
        for start in range(0, 4096, 512):
            here = slice(start, start + 512)
            value[:, here] = mm(d_high, held_ref[:, here]) + mm(d_low, held_ref[:, here])
        for row in range(4):
            for at in range(32):
                part_ref[32 * row + at] = value[8 * row : 8 * row + 8, 128 * at : 128 * at + 128]

    @pl.when(core == 1)
    def _():
        token_rows(come_ref, 0)
        part_ref[...] = jnp.zeros_like(part_ref)


def token_grads(at, *arrays):
    return pl.pallas_call(
        token_body,
        out_shape=(
            jax.ShapeDtypeStruct((256, 2048), bf16),
            jax.ShapeDtypeStruct((128, 8, 128), f32),
        ),
        in_specs=[smem_spec] + [vmem_spec] * 8,
        out_specs=(vmem_spec,) * 2,
        scratch_shapes=[pltpu.VMEM((32, 4096), f32)],
        compiler_params=roomy,
        cost_estimate=pl.CostEstimate(flops=1 << 29, bytes_accessed=6 << 20, transcendentals=0),
    )(at, *arrays)


def shards(tokens, cotangent, group_of, mixer, w_in, w_out):
    seqs, positions, width = tokens.shape
    rows = seqs * positions
    core = lax.axis_index("core")
    first = core == 0
    half = width // 2
    plane = lax.axis_index("z")
    at = jnp.stack(
        [core, own_step(core, plane)] + [piece_of(step, plane) for step in range(4)] + [plane]
    ).astype(jnp.int32)
    tie = lax.optimization_barrier

    home = group_of % 16
    earlier = jnp.arange(seqs)[:, None] > jnp.arange(seqs)[None, :]
    same = (home[:, None, :] == home[None, :, :]) & earlier[:, :, None]
    member = jnp.sum(same.astype(jnp.int32), axis=1)
    place = home * 8 + jnp.arange(positions, dtype=jnp.int32)[None, :] * 2 + member
    place = place.reshape(1, rows)
    packed = pack((0,), at, w_in, w_out)
    place, *packed = tie((place, *packed))
    sent = sort(place, tokens.reshape(rows, width), cotangent.reshape(rows, width))
    hot = (place == jnp.arange(rows, dtype=jnp.int32)[:, None]).astype(bf16)
    held = exchange(sent.reshape(16, 16, width), owners).reshape(256, width)

    def send_weights(step, piece):
        return lax.ppermute(piece, column, weight_round(step))

    weights = [send_weights(0, packed[0])]
    packed += pack((1,), at, w_in, w_out)
    weights[0], second = tie((weights[0], packed[1]))
    weights.append(send_weights(1, second))
    packed += pack((2, 3), at, w_in, w_out)

    planes = [(plane + d) % 4 for d in range(4)]
    mixer_e = mixer.T.reshape(8, 4, width)
    mixer_t = jnp.concatenate(
        [lax.dynamic_index_in_dim(mixer_e, p, 1, keepdims=False) for p in planes], axis=0
    )
    logits = mm(mixer_t, held, NT)
    logits = jnp.where(first, logits, lax.ppermute(logits, "core", swap))
    scaled = jnp.tanh(logits / soft_cap)
    exponent = jnp.exp(soft_cap * scaled)
    column_of = jnp.arange(256, dtype=jnp.int32) // 2 % 8
    mask = (column_of[None, :] == jnp.arange(8, dtype=jnp.int32)[:, None]).astype(f32)
    spread = exponent[:, None, :] * mask[None]
    spread = spread / jnp.sum(spread, axis=2, keepdims=True)
    spread_high, spread_low = split_high_low(spread)
    flat_high, flat_low = spread_high.reshape(256, 256), spread_low.reshape(256, 256)

    def shift(by):
        return [(s, (s + by) % 4) for s in range(4)]

    mix = (mm(flat_high, held) + mm(flat_low, held)).astype(bf16)
    mix, weights[1] = tie((mix, weights[1]))
    blocks = {}
    for d in (2, 1, 3, 0):
        block = mix[64 * d : 64 * d + 64]
        blocks[d] = lax.ppermute(block, "z", shift(d)) if d else block
    blocks[2], *later = tie((blocks[2], *packed[2:]))
    weights += [send_weights(step + 2, piece) for step, piece in enumerate(later)]
    sent = jnp.stack([blocks[d].reshape(8, 8, width) for d in range(4)], axis=1)
    sent = jnp.broadcast_to(sent[:, None], (8, 2, 4, 8, width)).reshape(16, 32, width)
    expert_rows = exchange(sent, near).reshape(8, 2, 4, 8, width)

    pre_act, given = up(at, expert_rows, weights, packed)
    got = lax.ppermute(given, "core", swap)
    part, units = down(at, pre_act, got, weights, packed)
    made = weight_grads(at, expert_rows, units)
    back = exchange(part.reshape(64, 8, width), same_core)

    def send_grads(step, piece):
        return lax.ppermute(piece, column, back_round(step))

    grads = [send_grads(0, made[0]), send_grads(1, made[1])]
    back, *later = tie((back, *made[2:]))

    def whole_order(array):
        split = array.reshape(4, 8, *array.shape[1:])
        order = [
            lax.dynamic_index_in_dim(split, (e - plane) % 4, 0, keepdims=False) for e in range(4)
        ]
        return jnp.stack(order, axis=1).reshape(array.shape)

    spread_e, scaled_e = whole_order(spread), whole_order(scaled)
    low, high, dots = sum_and_dots(back.reshape(32, 2, 8, width), held)
    come = lax.ppermute(low, "core", swap)
    dots_other = lax.ppermute(dots, "core", swap)
    grad_rows, mixer_part = token_grads(
        at, dots, dots_other, spread_e, scaled_e, high, come, mixer.T, held
    )
    grads.append(send_grads(2, later[0]))
    grad_rows = exchange(grad_rows.reshape(16, 16, half), owners)
    grad_rows, mixer_part, grads[0] = tie((grad_rows, mixer_part, grads[0]))
    pieces = exchange(mixer_part, axes)
    pieces, grads[1], grads[2], last = tie((pieces, grads[1], grads[2], later[1]))
    grads.append(send_grads(3, last))
    total = jnp.sum(pieces, axis=0, keepdims=True)
    whole = exchange(jnp.broadcast_to(total, (128, 8, 128)), axes)

    most = unpack((0, 1, 2), at, grads, made)
    grad_in, grad_out = unpack((3,), at, grads, made, most)
    grad_rows = grad_rows.reshape(8, 2, 16, half)
    grad_tokens = jnp.concatenate(
        [mm(hot, grad_rows[:, 1 - side].reshape(rows, half), TN).astype(bf16) for side in range(2)],
        axis=1,
    ).reshape(seqs, positions, width)
    whole, grad_in, grad_out = tie((whole, grad_in, grad_out))
    grad_mixer = whole.reshape(4, 32, 8, 128).transpose(1, 3, 0, 2).reshape(width, 32)
    return (grad_tokens, grad_mixer, grad_in, grad_out)


def solution(mesh):
    fine = Mesh(mesh.devices.reshape(sizes), axes)
    dp, expert = ("yh", "x", "core"), ("z", "b")
    every = dp + expert
    return jax.shard_map(
        shards,
        mesh=fine,
        in_specs=(
            P(every, None, None),
            P(every, None, None),
            P(every, None),
            P(),
            P(dp, None, expert),
            P(dp, expert, None),
        ),
        out_specs=(
            P(every, None, None),
            P(),
            P(dp, None, expert),
            P(dp, expert, None),
        ),
        check_vma=False,
    )
```
